512 devices in a mesh: team: 32 (over x_lo, z, core), member: 16 (over x_hi, y).
Axes of the slice: x: 4 (x_hi: 2, x_lo: 2; x = x_hi * 2 + x_lo), y: 8, z: 8, core: 2. Of those that a mesh axis runs over, the one named last changes fastest.
Arguments:
- feats: bfloat16 [65536, 128], P(('team', 'member')), may hold values from -6 to 6
- tile_weights: bfloat16 [32, 16, 16, 8, 128, 128], P('team', 'member'), may hold values from -6 to 6
- tile_rows: int32 [32, 16, 16, 8], P('team', 'member'), may hold values from 0 to 31, as said below
- slot_count: int32 [32, 16, 16], P('team', 'member'), may hold values from 1 to 8, as said below
- degrees: int32 [65536], P(('member', 'team')), may hold values from 2048 to 8192
- weight: bfloat16 [128, 256], replicated, may hold values from -0.5 to 0.5
- grad_out: bfloat16 [65536, 256], P(('member', 'team')), may hold values from -6 to 6
Outputs:
- out: bfloat16 [65536, 256], P(('member', 'team'))
- grad_weight: float32 [128, 256], replicated
- grad_feats: float32 [65536, 128], P(('team', 'member'))
The draws below stay inside these ranges and needn't reach their ends.
Inputs may be any that keep to these rules, and one draw needn't show every extreme that they name: `tile_rows`: within one column block of one device the 8 entries are distinct row blocks. `slot_count`: every device has a column block with all 8 slots live.
All inputs are finite; a program needn't handle non-finite values.
Results may differ from the reference program's by a relative error of at most 0.0049.
Values may be sent and summed in bfloat16 or wider, within the bound.
A program may use at most 64 MiB of HBM per device.

```python
import jax
import jax.numpy as jnp
from jax import lax

F = 128
HID = 256
BLOCK = 128
NPD = 128
RBLK = 32
CBLK = 16
SLOTS = 8
NODES = 65536
N_TEAM = 32
N_MEMBER = 16


def draw_tile_rows(key, part):
    key = jax.random.fold_in(key, 12)
    scores = jax.random.randint(key, (N_TEAM, N_MEMBER, CBLK, RBLK), 0, 65536, dtype=jnp.int32)
    scores = scores * RBLK + jnp.arange(RBLK, dtype=jnp.int32)
    ranked = jnp.argsort(scores, axis=-1, stable=True).astype(jnp.int32)
    return ranked[..., :SLOTS]


def draw_slot_count(key, part):
    key = jax.random.fold_in(key, 13)
    key_counts, key_full = jax.random.split(key)
    counts = jax.random.randint(key_counts, (N_TEAM, N_MEMBER, CBLK), 1, SLOTS + 1, dtype=jnp.int32)
    full_at = jax.random.randint(key_full, (N_TEAM, N_MEMBER, 1), 0, CBLK, dtype=jnp.int32)
    return jnp.where(jnp.arange(CBLK, dtype=jnp.int32) == full_at, SLOTS, counts).astype(jnp.int32)


def set_ends(array, key, smallest, top_value):
    longest = array.shape.index(max(array.shape))
    spots = []
    for shift in (0, 1):
        where = [jax.random.randint(jax.random.fold_in(key, axis), (), 0, length) for axis, length in enumerate(array.shape)]
        where[longest] = (where[longest] + shift) % array.shape[longest]
        spots.append(tuple(where))
    return array.at[spots[0]].set(smallest).at[spots[1]].set(top_value)


def block_levels(key, shape, shards, least, top_value):
    gain = 1.0
    for dim, blocks in shards:
        steps = jax.random.uniform(jax.random.fold_in(jax.random.fold_in(key, 6), dim), (blocks,), jnp.float32, least / len(shards), top_value / len(shards))
        gain = gain * jnp.repeat(jnp.exp(steps), shape[dim] // blocks).reshape((-1,) + (1,) * (len(shape) - 1 - dim))
    return gain


def bell_draw(rng, dims, scale, bound, cuts=(), held_as=jnp.bfloat16):
    values = scale * jax.random.normal(rng, dims, jnp.float32)
    if cuts:
        values = values * block_levels(rng, dims, cuts, -0.22, 0.18)
    return jnp.clip(values, -bound, bound).astype(held_as)


def setup_inputs(seed: int = 0) -> dict:
    arg_keys = jax.random.split(jax.random.key(seed), 8)
    feats = bell_draw(arg_keys[0], (NODES, F), 1.0, 6.0, ((0, 512),))
    tile_weights = bell_draw(arg_keys[1], (N_TEAM, N_MEMBER, CBLK, SLOTS, BLOCK, BLOCK), 1.0, 6.0, ((0, 32), (1, 16)))
    tile_rows = draw_tile_rows(jax.random.fold_in(arg_keys[7], 71), 0)
    slot_count = draw_slot_count(jax.random.fold_in(arg_keys[7], 71), 0)
    degrees = set_ends(jax.random.randint(arg_keys[4], (NODES,), N_TEAM * N_MEMBER * NPD // 32, N_TEAM * N_MEMBER * NPD // 8 + 1), jax.random.fold_in(arg_keys[4], 1), N_TEAM * N_MEMBER * NPD // 32, (N_TEAM * N_MEMBER * NPD // 8 + 1) - 1).astype(jnp.int32)
    weight = bell_draw(arg_keys[5], (F, HID), F ** -0.5, 0.5)
    grad_out = bell_draw(arg_keys[6], (NODES, HID), 1.0, 6.0, ((0, 512),))
    return dict(feats=feats, tile_weights=tile_weights, tile_rows=tile_rows, slot_count=slot_count, degrees=degrees, weight=weight, grad_out=grad_out)


def reference(feats, tile_weights, tile_rows, slot_count, degrees, weight, grad_out):
    highest = lax.Precision.HIGHEST
    live_mask = (jnp.arange(SLOTS, dtype=jnp.int32)[None, None, None, :] < slot_count[..., None]).astype(jnp.float32)
    team_feats = feats.astype(jnp.float32).reshape(N_TEAM, CBLK, BLOCK, F)

    def device_partial(team_id, member_id):

        def add_column(column, accumulated):
            tile_vals = tile_weights[team_id, member_id, column].astype(jnp.float32)
            products = jnp.einsum('sij,jf->sif', tile_vals, team_feats[team_id, column], precision=highest)
            products = products * live_mask[team_id, member_id, column][:, None, None]
            return accumulated.at[tile_rows[team_id, member_id, column]].add(products)
        return lax.fori_loop(0, CBLK, add_column, jnp.zeros((RBLK, BLOCK, F), jnp.float32))

    def member_rows(member_id):

        def over_team(accumulated, team_id):
            return (accumulated + device_partial(team_id, member_id), None)
        summed_rows, _ = lax.scan(over_team, jnp.zeros((RBLK, BLOCK, F), jnp.float32), jnp.arange(N_TEAM, dtype=jnp.int32))
        return summed_rows
    summed = lax.map(member_rows, jnp.arange(N_MEMBER, dtype=jnp.int32)).reshape(NODES, F)
    inv_root = lax.rsqrt(degrees.astype(jnp.float32))
    aggregate = (summed * inv_root[:, None]).astype(jnp.bfloat16)
    out = jnp.dot(aggregate, weight, preferred_element_type=jnp.float32).astype(jnp.bfloat16)
    grad_weight = jnp.dot(aggregate.T, grad_out, preferred_element_type=jnp.float32) * NODES ** (-0.5)
    scaled = (jnp.dot(grad_out, weight.T, preferred_element_type=jnp.float32) * inv_root[:, None]).astype(jnp.bfloat16)
    member_scaled = scaled.astype(jnp.float32).reshape(N_MEMBER, RBLK, BLOCK, F)

    def device_columns(team_id, member_id):

        def column_sum(column):
            tile_vals = tile_weights[team_id, member_id, column].astype(jnp.float32)
            picked = member_scaled[member_id][tile_rows[team_id, member_id, column]]
            picked = picked * live_mask[team_id, member_id, column][:, None, None]
            return jnp.einsum('sji,sjf->if', tile_vals, picked, precision=highest)
        return lax.map(column_sum, jnp.arange(CBLK, dtype=jnp.int32))

    def team_columns(team_id):

        def over_member(accumulated, member_id):
            return (accumulated + device_columns(team_id, member_id), None)
        column_rows, _ = lax.scan(over_member, jnp.zeros((CBLK, BLOCK, F), jnp.float32), jnp.arange(N_MEMBER, dtype=jnp.int32))
        return column_rows
    grad_feats = lax.map(team_columns, jnp.arange(N_TEAM, dtype=jnp.int32)).reshape(NODES, F)
    return (out, grad_weight, grad_feats)
```

```python
import jax
import jax.numpy as jnp
from jax import lax
from jax.experimental import pallas as pl
from jax.experimental.pallas import tpu as pltpu
from jax.sharding import PartitionSpec as P

MESH = pl.DeviceIdType.MESH
F32 = jnp.float32
BF16 = jnp.bfloat16

N_TEAM, N_MEMBER, N_CHIP = 32, 16, 16
BLOCK, FEAT, HID, SLOTS = 128, 128, 256, 8
COLS = 16
DEAD = COLS * SLOTS
SLAB = BLOCK // 8


def kernel(slot_of, row_of, feats, tiles_hbm, degrees, weight, grad_out,
           out, grad_weight, grad_feats,
           tiles, x_all, s_all, prod, from_sib, to_sib, own_part, to_team, from_team,
           to_member, from_member, gw_part, slab_in, slab, y_in, slab_y, z_in,
           tile_sem, x_send, x_recv, s_send, s_recv, f_send, f_recv, cs_send, cs_recv,
           t_send, t_recv, b_send, b_recv, g_send, g_recv, y_send, y_recv, z_send, z_recv,
           a_send, a_recv):
    t = lax.axis_index("team")
    m = lax.axis_index("member")
    core = lax.rem(t, 2)
    chip = t // 2
    z = lax.rem(chip, 8)
    x_lo = chip // 8
    y = lax.rem(m, 8)
    x_hi = m // 8
    sib = chip * 2 + 1 - core
    group = core + 2 * x_lo + 4 * x_hi

    def copy(src, dst, send, recv, team, member):
        return pltpu.make_async_remote_copy(
            src_ref=src, dst_ref=dst, send_sem=send, recv_sem=recv,
            device_id=(team, member), device_id_type=MESH)

    def member_peer(k):
        return lax.rem(m + k, N_MEMBER)

    def chip_peer(k):
        return lax.rem(chip + k, N_CHIP)

    def flip(j):
        c = 1 - core if j & 1 else core
        xl = 1 - x_lo if j & 2 else x_lo
        xh = 1 - x_hi if j & 4 else x_hi
        return (xl * 8 + z) * 2 + c, xh * 8 + y, c + 2 * xl + 4 * xh

    def tile_copy(c):
        return pltpu.make_async_copy(tiles_hbm.at[c], tiles.at[c], tile_sem.at[c])

    for c in range(COLS):
        tile_copy(c).start()

    barrier = pltpu.get_barrier_semaphore()

    @pl.loop(1, N_MEMBER)
    def _(k):
        pl.semaphore_signal(barrier, inc=1, device_id=(t, member_peer(k)), device_id_type=MESH)

    @pl.loop(1, N_CHIP)
    def _(k):
        pl.semaphore_signal(barrier, inc=1, device_id=(chip_peer(k) * 2 + core, m), device_id_type=MESH)

    pl.semaphore_signal(barrier, inc=1, device_id=(sib, m), device_id_type=MESH)
    for j in (3, 5, 6, 7):
        to_t, to_m, _ = flip(j)
        pl.semaphore_signal(barrier, inc=1, device_id=(to_t, to_m), device_id_type=MESH)

    inv_row = lax.rsqrt(degrees[...].astype(F32))
    scaled_t = lax.dot_general(weight[...], grad_out[...], (((1,), (1,)), ((), ())),
                               preferred_element_type=F32)
    s_all[t] = (scaled_t * inv_row).astype(BF16)
    s_all[N_TEAM] = jnp.zeros((FEAT, BLOCK), BF16)
    x_all[m] = feats[...]
    prod[DEAD] = jnp.zeros((BLOCK, FEAT), F32)
    inv_col = jnp.transpose(jnp.broadcast_to(inv_row, (BLOCK, BLOCK)))

    pl.semaphore_wait(barrier, 2 * 15 + 5)

    def x_copy(k):
        return copy(feats, x_all.at[m], x_send.at[k], x_recv.at[k], t, member_peer(k))

    def s_copy(k):
        return copy(s_all.at[t], s_all.at[t], s_send.at[k], s_recv.at[k], chip_peer(k) * 2 + core, m)

    def forward_copy(k):
        src = lax.rem(chip - k + N_CHIP, N_CHIP) * 2 + core
        return copy(s_all.at[src], s_all.at[src], f_send.at[k], f_recv.at[k], sib, m)

    forward_copy(0).start()

    @pl.loop(1, N_MEMBER)
    def _(k):
        x_copy(k).start()
        s_copy(k).start()

    for c in range(COLS):
        tile_copy(c).wait()

    def multiply(c):
        products = jnp.dot(tiles[c], x_all[c], preferred_element_type=F32)
        prod[pl.ds(c * SLOTS, SLOTS)] = products.reshape(SLOTS, BLOCK, FEAT)

    multiply(m)

    @pl.loop(1, N_MEMBER)
    def _(k):
        x_copy(k).wait_recv()
        multiply(lax.rem(m - k + N_MEMBER, N_MEMBER))
        s_copy(k).wait_recv()
        forward_copy(k).start()

    def row_sum(r):
        total = prod[slot_of[0, r]]
        for c in range(1, COLS):
            total = total + prod[slot_of[c, r]]
        return total

    def cs_copy(q):
        return copy(to_sib.at[q], from_sib.at[q], cs_send.at[q], cs_recv.at[q], sib, m)

    def t_copy(k):
        return copy(to_team.at[k], from_team.at[k], t_send.at[k], t_recv.at[k],
                    chip_peer(k) * 2 + core, m)

    @pl.loop(1, N_CHIP + 1)
    def _(k):
        q = chip_peer(k)
        to_sib[q] = row_sum(q * 2 + 1 - core).astype(BF16)
        cs_copy(q).start()

    @pl.loop(1, N_CHIP)
    def _(k):
        q = chip_peer(k)
        mine = row_sum(q * 2 + core)
        cs_copy(q).wait_recv()
        to_team[k] = (mine + from_sib[q].astype(F32)).astype(BF16)
        t_copy(k).start()

    mine = row_sum(t)
    cs_copy(chip).wait_recv()
    own_part[...] = mine + from_sib[chip].astype(F32)

    @pl.loop(0, N_CHIP)
    def _(k):
        src = lax.rem(chip - k + N_CHIP, N_CHIP) * 2 + 1 - core
        copy(s_all.at[src], s_all.at[src], f_send.at[k], f_recv.at[k], sib, m).wait_recv()

    def column(c):
        picked = jnp.concatenate([s_all[row_of[c, s]] for s in range(SLOTS)], axis=1)
        return jnp.dot(picked, tiles[c], preferred_element_type=F32)

    def b_copy(k):
        return copy(to_member.at[k], from_member.at[k], b_send.at[k], b_recv.at[k], t, member_peer(k))

    @pl.loop(1, N_MEMBER)
    def _(k):
        to_member[k] = column(member_peer(k)).astype(BF16)
        b_copy(k).start()

    own_col = column(m)

    @pl.loop(1, N_CHIP)
    def _(k):
        t_copy(k).wait_recv()

    summed = own_part[...]
    for k in range(1, N_CHIP):
        summed = summed + from_team[k].astype(F32)
    aggregate = (summed * inv_col).astype(BF16)
    gw_part[...] = lax.dot_general(aggregate, grad_out[...], (((0,), (0,)), ((), ())),
                                   preferred_element_type=F32).reshape(8, SLAB, HID)

    def g_copy(j):
        to_t, to_m, to_g = flip(j)
        return copy(gw_part.at[to_g], slab_in.at[j], g_send.at[j], g_recv.at[j], to_t, to_m)

    for j in range(1, 8):
        g_copy(j).start()

    out[...] = jnp.dot(aggregate, weight[...], preferred_element_type=F32).astype(BF16)

    for j in range(1, 8):
        g_copy(j).wait_recv()
    part = gw_part[group]
    for j in range(1, 8):
        part = part + slab_in[j]
    slab[...] = part

    def y_copy(k):
        return copy(slab, y_in.at[k], y_send.at[k], y_recv.at[k], t, x_hi * 8 + lax.rem(y + k, 8))

    def z_copy(k):
        return copy(slab_y, z_in.at[k], z_send.at[k], z_recv.at[k],
                    (x_lo * 8 + lax.rem(z + k, 8)) * 2 + core, m)

    for k in range(1, 8):
        y_copy(k).start()

    @pl.loop(1, N_MEMBER)
    def _(k):
        b_copy(k).wait_recv()

    for k in range(1, N_MEMBER):
        own_col = own_col + from_member[k].astype(F32)
    grad_feats[...] = jnp.transpose(own_col)

    for k in range(1, 8):
        y_copy(k).wait_recv()
    part = slab[...]
    for k in range(1, 8):
        part = part + y_in[k]
    slab_y[...] = part
    for k in range(1, 8):
        z_copy(k).start()
    for k in range(1, 8):
        z_copy(k).wait_recv()
    part = slab_y[...]
    for k in range(1, 8):
        part = part + z_in[k]
    grad_weight[group] = part * (N_TEAM * N_MEMBER * BLOCK) ** (-0.5)

    def a_copy(j):
        to_t, to_m, _ = flip(j)
        return copy(grad_weight.at[group], grad_weight.at[group], a_send.at[j], a_recv.at[j], to_t, to_m)

    for j in range(1, 8):
        a_copy(j).start()

    @pl.loop(1, N_MEMBER)
    def _(k):
        x_copy(k).wait_send()
        s_copy(k).wait_send()
        t_copy(k).wait_send()
        b_copy(k).wait_send()

    @pl.loop(0, N_CHIP)
    def _(k):
        forward_copy(k).wait_send()
        cs_copy(k).wait_send()

    for j in range(1, 8):
        g_copy(j).wait_send()
        y_copy(j).wait_send()
        z_copy(j).wait_send()
        a_copy(j).wait_send()
    for j in range(1, 8):
        a_copy(j).wait_recv()


def per_device(feats, tile_weights, tile_rows, slot_count, degrees, weight, grad_out):
    rows = tile_rows[0, 0]
    live = jnp.arange(SLOTS, dtype=jnp.int32)[None, :] < slot_count[0, 0][:, None]
    row_of = jnp.where(live, rows, N_TEAM)
    slot_ids = jnp.arange(COLS * SLOTS, dtype=jnp.int32).reshape(COLS, SLOTS)
    hit = row_of[:, None, :] == jnp.arange(N_TEAM, dtype=jnp.int32)[None, :, None]
    slot_of = jnp.min(jnp.where(hit, slot_ids[:, None, :], DEAD), axis=2)

    smem = pl.BlockSpec(memory_space=pltpu.SMEM)
    vmem = pl.BlockSpec(memory_space=pltpu.VMEM)
    hbm = pl.BlockSpec(memory_space=pl.ANY)
    dma = pltpu.SemaphoreType.DMA
    block = (BLOCK, FEAT)
    out, grad_weight, grad_feats = pl.pallas_call(
        kernel,
        out_shape=(
            jax.ShapeDtypeStruct((BLOCK, HID), BF16),
            jax.ShapeDtypeStruct((8, SLAB, HID), F32),
            jax.ShapeDtypeStruct((BLOCK, FEAT), F32),
        ),
        in_specs=[smem, smem, vmem, hbm, vmem, vmem, vmem],
        out_specs=(vmem, vmem, vmem),
        scratch_shapes=[
            pltpu.VMEM((COLS, SLOTS * BLOCK, BLOCK), BF16),
            pltpu.VMEM((COLS,) + block, BF16),
            pltpu.VMEM((N_TEAM + 1,) + block, BF16),
            pltpu.VMEM((DEAD + 1,) + block, F32),
            pltpu.VMEM((N_CHIP,) + block, BF16),
            pltpu.VMEM((N_CHIP,) + block, BF16),
            pltpu.VMEM(block, F32),
            pltpu.VMEM((N_CHIP,) + block, BF16),
            pltpu.VMEM((N_CHIP,) + block, BF16),
            pltpu.VMEM((N_MEMBER,) + block, BF16),
            pltpu.VMEM((N_MEMBER,) + block, BF16),
            pltpu.VMEM((8, SLAB, HID), F32),
            pltpu.VMEM((8, SLAB, HID), F32),
            pltpu.VMEM((SLAB, HID), F32),
            pltpu.VMEM((8, SLAB, HID), F32),
            pltpu.VMEM((SLAB, HID), F32),
            pltpu.VMEM((8, SLAB, HID), F32),
            dma((COLS,)),
            dma((16,)), dma((16,)), dma((16,)), dma((16,)), dma((16,)), dma((16,)), dma((16,)), dma((16,)),
            dma((16,)), dma((16,)), dma((16,)), dma((16,)), dma((8,)), dma((8,)), dma((8,)), dma((8,)),
            dma((8,)), dma((8,)), dma((8,)), dma((8,)),
        ],
        compiler_params=pltpu.CompilerParams(
            collective_id=0, has_side_effects=True, vmem_limit_bytes=62 * 1024 * 1024),
    )(
        slot_of, row_of, feats,
        tile_weights.reshape(COLS, SLOTS * BLOCK, BLOCK),
        degrees.reshape(1, BLOCK), weight, grad_out,
    )
    return out, grad_weight.reshape(BLOCK, HID), grad_feats


def solution(mesh):
    placed = (
        P(("team", "member"), None),
        P("team", "member", None, None, None, None),
        P("team", "member", None, None),
        P("team", "member", None),
        P(("member", "team")),
        P(),
        P(("member", "team"), None),
    )
    return jax.shard_map(
        per_device,
        mesh=mesh,
        in_specs=placed,
        out_specs=(P(("member", "team"), None), P(), P(("team", "member"), None)),
        check_vma=False,
    )
```

```python
import jax
import jax.numpy as jnp
from jax import lax
from jax.experimental import pallas as pl
from jax.experimental.pallas import tpu as pltpu
from jax.sharding import PartitionSpec as P

MESH = pl.DeviceIdType.MESH
F32 = jnp.float32
BF16 = jnp.bfloat16

N_TEAM, N_MEMBER, N_CHIP, RING = 32, 16, 16, 8
BLOCK, FEAT, HID, SLOTS = 128, 128, 256, 8
COLS = 16
HELD = SLOTS + 1
SLAB = BLOCK // 8
FAR, NEAR = (4, 3, 5), (6, 2, 7, 1)


def kernel(row_hbm, count_hbm, feats_hbm, tiles_hbm, degrees_hbm, weight_hbm, grad_out_hbm,
           out, grad_weight, grad_feats,
           slot_of, row_of, count, slot_vec, row_vec, count_vec, degrees, weight, grad_out,
           tiles, x_all, s_all, prod, from_sib, to_sib, own_part, to_team, from_team,
           to_member, from_member, gw_part, slab_out, slab_in, slab, y_in, slab_y, z_in,
           in_sem, slot_sem, tile_sem, x_send, x_recv, x2_send, x2_recv, s_send, s_recv, s2_send, s2_recv,
           f_send, f_recv, cs_send, cs_recv,
           t_send, t_recv, b_send, b_recv, g_send, g_recv, y_send, y_recv, z_send, z_recv,
           a_send, a_recv):
    t = lax.axis_index("team")
    m = lax.axis_index("member")
    core = lax.rem(t, 2)
    chip = t // 2
    z = lax.rem(chip, RING)
    x_lo = chip // RING
    y = lax.rem(m, RING)
    x_hi = m // RING
    sib = chip * 2 + 1 - core
    group = core + 2 * x_lo + 4 * x_hi

    def signal(team, member):
        pl.semaphore_signal(barrier, inc=1, device_id=(team, member), device_id_type=MESH)

    def copy(src, dst, send, recv, team, member):
        return pltpu.make_async_remote_copy(
            src_ref=src, dst_ref=dst, send_sem=send, recv_sem=recv,
            device_id=(team, member), device_id_type=MESH)

    def member_peer(k):
        return lax.rem(m + k, N_MEMBER)

    def chip_peer(k):
        return lax.rem(chip + k, N_CHIP)

    def flip(j):
        c = 1 - core if j & 1 else core
        xl = 1 - x_lo if j & 2 else x_lo
        xh = 1 - x_hi if j & 4 else x_hi
        return (xl * RING + z) * 2 + c, xh * RING + y, c + 2 * xl + 4 * xh

    def y_at(k):
        return lax.rem(y + k, RING)

    def z_at(k):
        return lax.rem(z + k, RING)

    def tile_copy(c):
        return pltpu.make_async_copy(tiles_hbm.at[c], tiles.at[c], tile_sem.at[c])

    pairs = ((weight_hbm, weight), (grad_out_hbm, grad_out), (degrees_hbm, degrees),
             (row_hbm, row_vec), (count_hbm, count_vec), (feats_hbm, x_all.at[m]),
             (row_hbm, row_of), (count_hbm, count))
    inputs = [pltpu.make_async_copy(src, dst, in_sem.at[i]) for i, (src, dst) in enumerate(pairs)]
    slot_copy = pltpu.make_async_copy(slot_vec, slot_of, slot_sem)

    barrier = pltpu.get_barrier_semaphore()

    @pl.loop(1, N_MEMBER)
    def _(k):
        signal(t, member_peer(k))
        signal(chip_peer(k) * 2 + core, m)

    signal(sib, m)
    for j in (3, 5, 6, 7):
        to_t, to_m, _ = flip(j)
        signal(to_t, to_m)

    for c in inputs:
        c.start()
    for c in range(COLS):
        tile_copy(c).start()

    pl.semaphore_wait(barrier, 2 * 15 + 5)

    def x_slot(row, k):
        return row * RING + lax.rem(y - k + RING, RING)

    def x_copy(k):
        return copy(feats_hbm, x_all.at[m], x_send.at[k], x_recv.at[k], t, x_hi * RING + y_at(k))

    def x_swap():
        return copy(feats_hbm, x_all.at[m], x2_send.at[0], x2_recv.at[0], t, (1 - x_hi) * RING + y)

    def x_near(k):
        slot = x_slot(1 - x_hi, 0)
        return copy(x_all.at[slot], x_all.at[slot], x2_send.at[k], x2_recv.at[k], t, x_hi * RING + y_at(k))

    def x_far(k):
        slot = x_slot(x_hi, k)
        return copy(x_all.at[slot], x_all.at[slot], x2_send.at[k], x2_recv.at[k], t, (1 - x_hi) * RING + y)

    def s_slot(row, k):
        return (row * RING + lax.rem(z - k + RING, RING)) * 2 + core

    def s_copy(k):
        return copy(s_all.at[t], s_all.at[t], s_send.at[k], s_recv.at[k], (x_lo * RING + z_at(k)) * 2 + core, m)

    def s_swap():
        return copy(s_all.at[t], s_all.at[t], s2_send.at[0], s2_recv.at[0], ((1 - x_lo) * RING + z) * 2 + core, m)

    def s_near(k):
        slot = s_slot(1 - x_lo, 0)
        return copy(s_all.at[slot], s_all.at[slot], s2_send.at[k], s2_recv.at[k],
                    (x_lo * RING + z_at(k)) * 2 + core, m)

    def s_far(k):
        slot = s_slot(x_lo, k)
        return copy(s_all.at[slot], s_all.at[slot], s2_send.at[k], s2_recv.at[k],
                    ((1 - x_lo) * RING + z) * 2 + core, m)

    def pass_on(row, k):
        slot = s_slot(x_lo if row == 0 else 1 - x_lo, k)
        return copy(s_all.at[slot], s_all.at[slot], f_send.at[row * RING + k], f_recv.at[row * RING + k], sib, m)

    def passed(row, k):
        slot = s_slot(x_lo if row == 0 else 1 - x_lo, k) + 1 - 2 * core
        return copy(s_all.at[slot], s_all.at[slot], f_send.at[row * RING + k], f_recv.at[row * RING + k], sib, m)

    x_swap().start()
    for k in FAR + NEAR:
        x_copy(k).start()

    for c in inputs[:3]:
        c.wait()
    inv_row = lax.rsqrt(degrees[...].astype(F32))
    scaled_t = lax.dot_general(weight[...], grad_out[...], (((1,), (1,)), ((), ())),
                               preferred_element_type=F32)
    s_all[t] = (scaled_t * inv_row).astype(BF16)
    s_swap().start()
    for k in FAR + NEAR:
        s_copy(k).start()
    pass_on(0, 0).start()

    for c in inputs[3:]:
        c.wait()
    row_ids = lax.broadcasted_iota(jnp.int32, (N_TEAM, COLS), 0)
    slots = jnp.full((N_TEAM, COLS), SLOTS, jnp.int32)
    for s in range(SLOTS):
        slots = jnp.where((row_vec[s:s + 1, :] == row_ids) & (s < count_vec[...]), s, slots)
    slot_vec[...] = slots
    slot_copy.start()

    s_all[N_TEAM] = jnp.zeros((FEAT, BLOCK), BF16)
    for c in range(COLS):
        prod[c * HELD + SLOTS] = jnp.zeros((BLOCK, FEAT), F32)
    inv_col = jnp.transpose(jnp.broadcast_to(inv_row, (BLOCK, BLOCK)))
    for c in range(COLS):
        tile_copy(c).wait()
    slot_copy.wait()

    def multiply(c):
        products = jnp.dot(tiles[c], x_all[c], preferred_element_type=F32)
        prod[pl.ds(c * HELD, SLOTS)] = products.reshape(SLOTS, BLOCK, FEAT)

    x_swap().wait_recv()
    for k in NEAR:
        x_near(k).start()
    s_swap().wait_recv()
    for k in NEAR:
        s_near(k).start()
    pass_on(1, 0).start()
    multiply(m)
    multiply(x_slot(1 - x_hi, 0))
    for k in FAR:
        x_copy(k).wait_recv()
        x_far(k).start()
        s_copy(k).wait_recv()
        s_far(k).start()
        pass_on(0, k).start()
    for k in FAR:
        multiply(x_slot(x_hi, k))
    for k in NEAR:
        x_copy(k).wait_recv()
        multiply(x_slot(x_hi, k))
    for k in NEAR:
        s_copy(k).wait_recv()
        pass_on(0, k).start()
    for k in NEAR:
        x_near(k).wait_recv()
        multiply(x_slot(1 - x_hi, k))
    for k in FAR:
        x_far(k).wait_recv()
        multiply(x_slot(1 - x_hi, k))

    def row_sum(r):
        total = prod[slot_of[r, 0]]
        for c in range(1, COLS):
            total = total + prod[c * HELD + slot_of[r, c]]
        return total

    def outward(i):
        return lax.rem(4 + ((i + 1) // 2) * (1 - 2 * lax.rem(i, 2)) + RING, RING)

    def cs_copy(q):
        return copy(to_sib.at[q], from_sib.at[q], cs_send.at[q], cs_recv.at[q], sib, m)

    def t_copy(k):
        return copy(to_team.at[k], from_team.at[k], t_send.at[k], t_recv.at[k],
                    chip_peer(k) * 2 + core, m)

    def for_sibling(q):
        to_sib[q] = row_sum(q * 2 + 1 - core).astype(BF16)
        cs_copy(q).start()

    def for_team(q):
        mine = row_sum(q * 2 + core)
        cs_copy(q).wait_recv()
        k = lax.rem(q - chip + N_CHIP, N_CHIP)
        to_team[k] = (mine + from_sib[q].astype(F32)).astype(BF16)
        t_copy(k).start()

    @pl.loop(0, RING)
    def _(i):
        dz = z_at(outward(i))
        for_sibling((1 - x_lo) * RING + dz)
        for_sibling(x_lo * RING + dz)

    @pl.loop(0, RING - 1)
    def _(i):
        dz = z_at(outward(i))
        for_team((1 - x_lo) * RING + dz)
        for_team(x_lo * RING + dz)

    for_team((1 - x_lo) * RING + z)
    mine = row_sum(t)
    cs_copy(chip).wait_recv()
    own_part[...] = mine + from_sib[chip].astype(F32)

    for k in NEAR:
        s_near(k).wait_recv()
        pass_on(1, k).start()
    for k in FAR:
        s_far(k).wait_recv()
        pass_on(1, k).start()

    @pl.loop(0, RING)
    def _(k):
        passed(0, k).wait_recv()
        passed(1, k).wait_recv()

    def column(c):
        picked = [s_all[jnp.where(s < count[0, c], row_of[s, c], N_TEAM)] for s in range(SLOTS)]
        return jnp.dot(jnp.concatenate(picked, axis=1), tiles[c], preferred_element_type=F32)

    def b_copy(k):
        return copy(to_member.at[k], from_member.at[k], b_send.at[k], b_recv.at[k], t, member_peer(k))

    def for_member(c):
        k = lax.rem(c - m + N_MEMBER, N_MEMBER)
        to_member[k] = column(c).astype(BF16)
        b_copy(k).start()

    @pl.loop(0, RING - 1)
    def _(i):
        dy = y_at(outward(i))
        for_member((1 - x_hi) * RING + dy)
        for_member(x_hi * RING + dy)

    for_member((1 - x_hi) * RING + y)
    own_col = column(m)

    @pl.loop(1, N_CHIP)
    def _(k):
        t_copy(k).wait_recv()

    summed = own_part[...]
    for k in range(1, N_CHIP):
        summed = summed + from_team[k].astype(F32)
    aggregate = (summed * inv_col).astype(BF16)
    part = lax.dot_general(aggregate, grad_out[...], (((0,), (0,)), ((), ())),
                           preferred_element_type=F32).reshape(8, SLAB, HID)
    gw_part[...] = part
    slab_out[...] = part.astype(BF16)

    def g_copy(j):
        to_t, to_m, to_g = flip(j)
        return copy(slab_out.at[to_g], slab_in.at[j], g_send.at[j], g_recv.at[j], to_t, to_m)

    for j in (7, 6, 5, 4, 3, 2, 1):
        g_copy(j).start()

    out[...] = jnp.dot(aggregate, weight[...], preferred_element_type=F32).astype(BF16)

    for j in range(1, 8):
        g_copy(j).wait_recv()
    part = gw_part[group]
    for j in range(1, 8):
        part = part + slab_in[j].astype(F32)
    slab[...] = part.astype(BF16)

    def y_copy(k):
        return copy(slab, y_in.at[k], y_send.at[k], y_recv.at[k], t, x_hi * RING + y_at(k))

    def z_copy(k):
        return copy(slab_y, z_in.at[k], z_send.at[k], z_recv.at[k], (x_lo * RING + z_at(k)) * 2 + core, m)

    for k in FAR + NEAR:
        y_copy(k).start()

    @pl.loop(1, N_MEMBER)
    def _(k):
        b_copy(k).wait_recv()

    for k in range(1, N_MEMBER):
        own_col = own_col + from_member[k].astype(F32)
    grad_feats[...] = jnp.transpose(own_col)

    for k in range(1, RING):
        y_copy(k).wait_recv()
    for k in range(1, RING):
        part = part + y_in[k].astype(F32)
    slab_y[...] = part.astype(BF16)
    for k in FAR + NEAR:
        z_copy(k).start()
    for k in range(1, RING):
        z_copy(k).wait_recv()
    part = slab_y[...].astype(F32)
    for k in range(1, RING):
        part = part + z_in[k].astype(F32)
    grad_weight[group] = part * (N_TEAM * N_MEMBER * BLOCK) ** (-0.5)

    def a_copy(j):
        to_t, to_m, _ = flip(j)
        return copy(grad_weight.at[group], grad_weight.at[group], a_send.at[j], a_recv.at[j], to_t, to_m)

    for j in (7, 6, 5, 4, 3, 2, 1):
        a_copy(j).start()

    @pl.loop(1, N_MEMBER)
    def _(k):
        t_copy(k).wait_send()
        b_copy(k).wait_send()

    @pl.loop(0, N_CHIP)
    def _(k):
        cs_copy(k).wait_send()

    @pl.loop(1, RING)
    def _(k):
        x_copy(k).wait_send()
        s_copy(k).wait_send()

    x_swap().wait_send()
    s_swap().wait_send()
    for k in NEAR:
        x_near(k).wait_send()
        s_near(k).wait_send()
    for k in FAR:
        x_far(k).wait_send()
        s_far(k).wait_send()

    @pl.loop(0, RING)
    def _(k):
        pass_on(0, k).wait_send()
        pass_on(1, k).wait_send()

    for j in range(1, 8):
        g_copy(j).wait_send()
        y_copy(j).wait_send()
        z_copy(j).wait_send()
        a_copy(j).wait_send()
    for j in range(1, 8):
        a_copy(j).wait_recv()


def place(out, grad_weight, grad_feats, to_out, to_weight, to_feats, held_out, held_weight, held_feats, sem):
    held = (held_out, held_weight, held_feats)
    inward = [pltpu.make_async_copy(src, dst, sem.at[i]) for i, (src, dst) in enumerate(zip((out, grad_weight, grad_feats), held))]
    outward = [pltpu.make_async_copy(src, dst, sem.at[i]) for i, (src, dst) in enumerate(zip(held, (to_out, to_weight, to_feats)))]
    for c in inward:
        c.start()
    for c, d in zip(inward, outward):
        c.wait()
        d.start()
    for d in outward:
        d.wait()


def per_device(feats, tile_weights, tile_rows, slot_count, degrees, weight, grad_out):
    rows = tile_rows[0, 0].T
    count = slot_count.reshape(1, COLS)
    vmem = pl.BlockSpec(memory_space=pltpu.VMEM)
    hbm = pl.BlockSpec(memory_space=pl.ANY)
    dma = pltpu.SemaphoreType.DMA
    block = (BLOCK, FEAT)
    out_shape = (
        jax.ShapeDtypeStruct((BLOCK, HID), BF16),
        jax.ShapeDtypeStruct((8, SLAB, HID), F32),
        jax.ShapeDtypeStruct((BLOCK, FEAT), F32),
    )
    results = pl.pallas_call(
        kernel,
        out_shape=out_shape,
        in_specs=[hbm] * 7,
        out_specs=(vmem, vmem, vmem),
        scratch_shapes=[
            pltpu.SMEM((N_TEAM, COLS), jnp.int32),
            pltpu.SMEM((SLOTS, COLS), jnp.int32),
            pltpu.SMEM((1, COLS), jnp.int32),
            pltpu.VMEM((N_TEAM, COLS), jnp.int32),
            pltpu.VMEM((SLOTS, COLS), jnp.int32),
            pltpu.VMEM((1, COLS), jnp.int32),
            pltpu.VMEM((1, BLOCK), jnp.int32),
            pltpu.VMEM((FEAT, HID), BF16),
            pltpu.VMEM((BLOCK, HID), BF16),
            pltpu.VMEM((COLS, SLOTS * BLOCK, BLOCK), BF16),
            pltpu.VMEM((COLS,) + block, BF16),
            pltpu.VMEM((N_TEAM + 1,) + block, BF16),
            pltpu.VMEM((COLS * HELD,) + block, F32),
            pltpu.VMEM((N_CHIP,) + block, BF16),
            pltpu.VMEM((N_CHIP,) + block, BF16),
            pltpu.VMEM(block, F32),
            pltpu.VMEM((N_CHIP,) + block, BF16),
            pltpu.VMEM((N_CHIP,) + block, BF16),
            pltpu.VMEM((N_MEMBER,) + block, BF16),
            pltpu.VMEM((N_MEMBER,) + block, BF16),
            pltpu.VMEM((8, SLAB, HID), F32),
            pltpu.VMEM((8, SLAB, HID), BF16),
            pltpu.VMEM((8, SLAB, HID), BF16),
            pltpu.VMEM((SLAB, HID), BF16),
            pltpu.VMEM((8, SLAB, HID), BF16),
            pltpu.VMEM((SLAB, HID), BF16),
            pltpu.VMEM((8, SLAB, HID), BF16),
            dma((8,)), dma, dma((COLS,)),
            dma((8,)), dma((8,)), dma((8,)), dma((8,)), dma((8,)), dma((8,)), dma((8,)), dma((8,)),
            dma((16,)), dma((16,)), dma((16,)), dma((16,)),
            dma((16,)), dma((16,)), dma((16,)), dma((16,)), dma((8,)), dma((8,)), dma((8,)), dma((8,)),
            dma((8,)), dma((8,)), dma((8,)), dma((8,)),
        ],
        compiler_params=pltpu.CompilerParams(
            collective_id=0, has_side_effects=True, vmem_limit_bytes=60 * 1024 * 1024),
    )(
        rows, count, feats,
        tile_weights.reshape(COLS, SLOTS * BLOCK, BLOCK),
        degrees.reshape(1, BLOCK), weight, grad_out,
    )
    out, grad_weight, grad_feats = pl.pallas_call(
        place,
        out_shape=out_shape,
        in_specs=[hbm] * 3,
        out_specs=(hbm,) * 3,
        scratch_shapes=[pltpu.VMEM(o.shape, o.dtype) for o in out_shape] + [dma((3,))],
    )(*results)
    return out, grad_weight.reshape(BLOCK, HID), grad_feats


def solution(mesh):
    placed = (
        P(("team", "member"), None),
        P("team", "member", None, None, None, None),
        P("team", "member", None, None),
        P("team", "member", None),
        P(("member", "team")),
        P(),
        P(("member", "team"), None),
    )
    return jax.shard_map(
        per_device,
        mesh=mesh,
        in_specs=placed,
        out_specs=(P(("member", "team"), None), P(), P(("team", "member"), None)),
        check_vma=False,
    )
```

```python
import jax
import jax.numpy as jnp
from jax import lax
from jax.experimental import pallas as pl
from jax.experimental.pallas import tpu as pltpu
from jax.sharding import PartitionSpec as P

MESH = pl.DeviceIdType.MESH
F32 = jnp.float32
BF16 = jnp.bfloat16

N_TEAM, N_MEMBER, N_CHIP, RING = 32, 16, 16, 8
BLOCK, FEAT, HID, SLOTS = 128, 128, 256, 8
COLS = 16
HELD = SLOTS + 1
SLAB = BLOCK // 8
FAR, NEAR = (4, 3, 5), (6, 2, 7, 1)
SPLIT = 4


def kernel(row_hbm, count_hbm, feats_hbm, tiles_hbm, degrees_hbm, weight_hbm, grad_out_hbm,
           out, grad_weight, grad_feats,
           slot_of, row_of, count, slot_vec, row_vec, count_vec, deg_all, weight, g_all, q_t,
           tiles, x_all, s_all, prod, from_sib, to_sib, own_part, to_team, from_team,
           to_bx, from_bx, held_b, to_member, from_member, gw_part, slab_out, slab_in, slab, y_in, slab_y, z_in,
           in_sem, slot_sem, tile_sem, x_send, x_recv, x2_send, x2_recv, c_send, c_recv, c2_send, c2_recv, d_send, d_recv,
           f_send, f_recv, cs_send, cs_recv,
           t_send, t_recv, bx_send, bx_recv, b_send, b_recv, g_send, g_recv, y_send, y_recv, z_send, z_recv,
           a_send, a_recv):
    t = lax.axis_index("team")
    m = lax.axis_index("member")
    core = lax.rem(t, 2)
    chip = t // 2
    z = lax.rem(chip, RING)
    x_lo = chip // RING
    y = lax.rem(m, RING)
    x_hi = m // RING
    sib = chip * 2 + 1 - core
    group = core + 2 * x_lo + 4 * x_hi

    def signal(team, member):
        pl.semaphore_signal(barrier, inc=1, device_id=(team, member), device_id_type=MESH)

    def copy(src, dst, send, recv, team, member):
        return pltpu.make_async_remote_copy(
            src_ref=src, dst_ref=dst, send_sem=send, recv_sem=recv,
            device_id=(team, member), device_id_type=MESH)

    def chip_peer(k):
        return lax.rem(chip + k, N_CHIP)

    def flip(j):
        c = 1 - core if j & 1 else core
        xl = 1 - x_lo if j & 2 else x_lo
        xh = 1 - x_hi if j & 4 else x_hi
        return (xl * RING + z) * 2 + c, xh * RING + y, c + 2 * xl + 4 * xh

    def y_at(k):
        return lax.rem(y + k, RING)

    def z_at(k):
        return lax.rem(z + k, RING)

    def tile_copy(c):
        part = pl.ds(c * 4, 4)
        return pltpu.make_async_copy(tiles_hbm.at[part], tiles.at[part], tile_sem.at[c])

    pairs = ((weight_hbm, weight), (grad_out_hbm, g_all.at[chip]), (degrees_hbm, deg_all.at[chip]),
             (row_hbm, row_vec), (count_hbm, count_vec), (feats_hbm, x_all.at[m]),
             (row_hbm, row_of), (count_hbm, count))
    inputs = [pltpu.make_async_copy(src, dst, in_sem.at[i]) for i, (src, dst) in enumerate(pairs)]
    slot_copy = pltpu.make_async_copy(slot_vec, slot_of, slot_sem)

    barrier = pltpu.get_barrier_semaphore()

    for k in FAR + NEAR:
        signal(t, x_hi * RING + y_at(k))
    signal(t, (1 - x_hi) * RING + y)

    @pl.loop(1, N_CHIP)
    def _(k):
        signal(chip_peer(k) * 2 + core, m)

    signal(sib, m)
    for j in (3, 5, 6, 7):
        to_t, to_m, _ = flip(j)
        signal(to_t, to_m)

    pl.semaphore_wait(barrier, RING + N_CHIP - 1 + 5)

    def x_slot(row, k):
        return row * RING + lax.rem(y - k + RING, RING)

    def x_copy(k):
        return copy(feats_hbm, x_all.at[m], x_send.at[k], x_recv.at[k], t, x_hi * RING + y_at(k))

    def x_swap():
        return copy(feats_hbm, x_all.at[m], x2_send.at[0], x2_recv.at[0], t, (1 - x_hi) * RING + y)

    def x_near(k):
        slot = x_slot(1 - x_hi, 0)
        return copy(x_all.at[slot], x_all.at[slot], x2_send.at[k], x2_recv.at[k], t, x_hi * RING + y_at(k))

    def x_far(k):
        slot = x_slot(x_hi, k)
        return copy(x_all.at[slot], x_all.at[slot], x2_send.at[k], x2_recv.at[k], t, (1 - x_hi) * RING + y)

    def c_slot(row, k):
        return row * RING + lax.rem(z - k + RING, RING)

    def c_copy(k):
        return copy(grad_out_hbm, g_all.at[chip], c_send.at[k], c_recv.at[k], (x_lo * RING + z_at(k)) * 2 + core, m)

    def c_relay(k):
        back, to = {3: (2, 1), 4: (2, 2), 5: (6, 7)}[k]
        slot = c_slot(x_lo, back)
        return copy(g_all.at[slot], g_all.at[slot], c_send.at[k], c_recv.at[k],
                    (x_lo * RING + z_at(to)) * 2 + core, m)

    def c_swap():
        return copy(grad_out_hbm, g_all.at[chip], c2_send.at[0], c2_recv.at[0], ((1 - x_lo) * RING + z) * 2 + core, m)

    def c_near(k):
        slot = c_slot(1 - x_lo, 0)
        return copy(g_all.at[slot], g_all.at[slot], c2_send.at[k], c2_recv.at[k],
                    (x_lo * RING + z_at(k)) * 2 + core, m)

    def c_far(k):
        slot = c_slot(x_lo, k)
        return copy(g_all.at[slot], g_all.at[slot], c2_send.at[k], c2_recv.at[k],
                    ((1 - x_lo) * RING + z) * 2 + core, m)

    def d_copy(k):
        return copy(degrees_hbm, deg_all.at[chip], d_send.at[k], d_recv.at[k], chip_peer(k) * 2 + core, m)

    def inv_root(q):
        return lax.rsqrt(deg_all[q].astype(F32))

    def pass_on(q):
        r = q * 2 + core
        return copy(s_all.at[r], s_all.at[r], f_send.at[q], f_recv.at[q], sib, m)

    def passed(q):
        r = q * 2 + 1 - core
        return copy(s_all.at[r], s_all.at[r], f_send.at[q], f_recv.at[q], sib, m)

    def project(q):
        scaled_t = lax.dot_general(weight[...], g_all[q], (((1,), (1,)), ((), ())), preferred_element_type=F32)
        s_all[q * 2 + core] = (scaled_t * inv_root(q)).astype(BF16)
        pass_on(q).start()

    x_swap().start()
    for k in FAR + NEAR:
        x_copy(k).start()
    c_swap().start()
    for k in NEAR:
        c_copy(k).start()
    for c in inputs:
        c.start()
    for c in range(COLS // 4):
        tile_copy(c).start()

    @pl.loop(1, N_CHIP)
    def _(k):
        d_copy(k).start()

    for c in inputs:
        c.wait()
    row_ids = lax.broadcasted_iota(jnp.int32, (N_TEAM, COLS), 0)
    slots = jnp.full((N_TEAM, COLS), SLOTS, jnp.int32)
    for s in range(SLOTS):
        slots = jnp.where((row_vec[s:s + 1, :] == row_ids) & (s < count_vec[...]), s, slots)
    slot_vec[...] = slots
    slot_copy.start()

    s_all[N_TEAM] = jnp.zeros((FEAT, BLOCK), BF16)
    for c in range(COLS):
        prod[c * HELD + SLOTS] = jnp.zeros((BLOCK, FEAT), F32)
    for c in range(COLS // 4):
        tile_copy(c).wait()
    slot_copy.wait()

    def multiply(c):
        products = jnp.dot(tiles[c], x_all[c], preferred_element_type=F32)
        prod[pl.ds(c * HELD, SLOTS)] = products.reshape(SLOTS, BLOCK, FEAT)

    x_swap().wait_recv()
    for k in NEAR:
        x_near(k).start()
    multiply(m)
    multiply(x_slot(1 - x_hi, 0))
    for k in FAR:
        x_copy(k).wait_recv()
        x_far(k).start()
    c_swap().wait_recv()
    for k in (6, 2):
        c_copy(k).wait_recv()
    for k in FAR:
        c_relay(k).start()
    for k in NEAR:
        c_near(k).start()
    for k in FAR:
        multiply(x_slot(x_hi, k))
    for k in NEAR:
        x_copy(k).wait_recv()
        multiply(x_slot(x_hi, k))

    @pl.loop(1, N_CHIP)
    def _(k):
        d_copy(k).wait_recv()

    project(chip)
    for k in NEAR:
        x_near(k).wait_recv()
        multiply(x_slot(1 - x_hi, k))
    for k in FAR:
        x_far(k).wait_recv()
        c_relay(k).wait_recv()
        c_far(k).start()
        multiply(x_slot(1 - x_hi, k))

    def row_sum(r):
        total = prod[slot_of[r, 0]]
        for c in range(1, COLS):
            total = total + prod[c * HELD + slot_of[r, c]]
        return total

    def outward(i):
        return lax.rem(4 + ((i + 1) // 2) * (1 - 2 * lax.rem(i, 2)) + RING, RING)

    def cs_copy(q):
        return copy(to_sib.at[q], from_sib.at[q], cs_send.at[q], cs_recv.at[q], sib, m)

    def t_copy(k):
        return copy(to_team.at[k], from_team.at[k], t_send.at[k], t_recv.at[k],
                    chip_peer(k) * 2 + core, m)

    def for_sibling(q):
        to_sib[q] = row_sum(q * 2 + 1 - core).astype(BF16)
        cs_copy(q).start()

    def finish_block(q):
        mine = row_sum(q * 2 + core)
        cs_copy(q).wait_recv()
        total = mine + from_sib[q].astype(F32)
        q_t[q] = (jnp.transpose(total) * inv_root(q)).astype(BF16)
        return total

    def for_team(q):
        k = lax.rem(q - chip + N_CHIP, N_CHIP)
        to_team[k] = finish_block(q).astype(BF16)
        t_copy(k).start()

    @pl.loop(0, RING)
    def _(i):
        dz = z_at(outward(i))
        for_sibling((1 - x_lo) * RING + dz)
        for_sibling(x_lo * RING + dz)

    @pl.loop(0, RING - 1)
    def _(i):
        dz = z_at(outward(i))
        for_team((1 - x_lo) * RING + dz)
        for_team(x_lo * RING + dz)

    for_team((1 - x_lo) * RING + z)
    own_part[...] = finish_block(chip)

    for k in (7, 1):
        c_copy(k).wait_recv()

    def weight_part(row):
        first = row * RING
        return jnp.dot(jnp.concatenate([q_t[first + i] for i in range(RING)], axis=1),
                       g_all[pl.ds(first, RING)].reshape(RING * BLOCK, HID), preferred_element_type=F32)

    part = weight_part(x_lo)
    for k in FAR + NEAR:
        project(c_slot(x_lo, k))
    project(c_slot(1 - x_lo, 0))
    for k in NEAR:
        c_near(k).wait_recv()
    for k in FAR:
        c_far(k).wait_recv()
    part = (part + weight_part(1 - x_lo)).reshape(8, SLAB, HID)
    gw_part[...] = part
    slab_out[...] = part.astype(BF16)

    def g_copy(j):
        to_t, to_m, to_g = flip(j)
        return copy(slab_out.at[to_g], slab_in.at[j], g_send.at[j], g_recv.at[j], to_t, to_m)

    for j in (7, 6, 5, 4, 3, 2, 1):
        g_copy(j).start()

    for k in FAR + NEAR:
        project(c_slot(1 - x_lo, k))

    for j in range(1, 8):
        g_copy(j).wait_recv()
    part = gw_part[group]
    for j in range(1, 8):
        part = part + slab_in[j].astype(F32)
    slab[...] = part.astype(BF16)

    def y_copy(k):
        return copy(slab, y_in.at[k], y_send.at[k], y_recv.at[k], t, x_hi * RING + y_at(k))

    def z_copy(k):
        return copy(slab_y, z_in.at[k], z_send.at[k], z_recv.at[k], (x_lo * RING + z_at(k)) * 2 + core, m)

    for k in FAR + NEAR:
        y_copy(k).start()

    @pl.loop(0, N_CHIP)
    def _(q):
        passed(q).wait_recv()

    def column(c):
        picked = [s_all[jnp.where(s < count[0, c], row_of[s, c], N_TEAM)] for s in range(SLOTS)]
        return jnp.dot(jnp.concatenate(picked, axis=1), tiles[c], preferred_element_type=F32)

    def bx_copy(i):
        return copy(to_bx.at[i], from_bx.at[i], bx_send.at[i], bx_recv.at[i], t, (1 - x_hi) * RING + y)

    def b_copy(k):
        return copy(to_member.at[k], from_member.at[k], b_send.at[k], b_recv.at[k], t, x_hi * RING + y_at(k))

    @pl.loop(0, RING)
    def _(i):
        dy = y_at(outward(i))
        to_bx[dy] = column((1 - x_hi) * RING + dy).astype(BF16)
        bx_copy(dy).start()

    @pl.loop(0, RING)
    def _(i):
        dy = y_at(outward(i))
        held_b[dy] = column(x_hi * RING + dy)

    def for_member(i):
        k = outward(i)
        dy = y_at(k)
        bx_copy(dy).wait_recv()
        to_member[k] = (held_b[dy] + from_bx[dy].astype(F32)).astype(BF16)
        b_copy(k).start()

    pl.loop(0, SPLIT)(for_member)

    for k in range(1, RING):
        y_copy(k).wait_recv()
    for k in range(1, RING):
        part = part + y_in[k].astype(F32)
    slab_y[...] = part.astype(BF16)
    for k in FAR + NEAR:
        z_copy(k).start()
    pl.loop(SPLIT, RING - 1)(for_member)

    @pl.loop(1, N_CHIP)
    def _(k):
        t_copy(k).wait_recv()

    summed = own_part[...]
    for k in range(1, N_CHIP):
        summed = summed + from_team[k].astype(F32)
    inv_col = jnp.transpose(jnp.broadcast_to(inv_root(chip), (BLOCK, BLOCK)))
    aggregate = (summed * inv_col).astype(BF16)
    out[...] = jnp.dot(aggregate, weight[...], preferred_element_type=F32).astype(BF16)

    for k in range(1, RING):
        z_copy(k).wait_recv()
    part = slab_y[...].astype(F32)
    for k in range(1, RING):
        part = part + z_in[k].astype(F32)
    grad_weight[group] = part * (N_TEAM * N_MEMBER * BLOCK) ** (-0.5)

    def a_copy(j):
        to_t, to_m, _ = flip(j)
        return copy(grad_weight.at[group], grad_weight.at[group], a_send.at[j], a_recv.at[j], to_t, to_m)

    for j in (7, 6, 5, 4, 3, 2, 1):
        a_copy(j).start()

    bx_copy(y).wait_recv()
    own_col = held_b[y] + from_bx[y].astype(F32)
    for k in FAR + NEAR:
        b_copy(k).wait_recv()
        own_col = own_col + from_member[k].astype(F32)
    grad_feats[...] = jnp.transpose(own_col)

    @pl.loop(1, N_MEMBER)
    def _(k):
        t_copy(k).wait_send()
        d_copy(k).wait_send()

    @pl.loop(0, N_CHIP)
    def _(k):
        cs_copy(k).wait_send()

    @pl.loop(0, RING)
    def _(k):
        bx_copy(k).wait_send()

    @pl.loop(1, RING)
    def _(k):
        b_copy(k).wait_send()
        x_copy(k).wait_send()

    x_swap().wait_send()
    c_swap().wait_send()
    for k in NEAR:
        x_near(k).wait_send()
        c_near(k).wait_send()
        c_copy(k).wait_send()
    for k in FAR:
        x_far(k).wait_send()
        c_far(k).wait_send()
        c_relay(k).wait_send()

    @pl.loop(0, RING)
    def _(k):
        pass_on(k).wait_send()
        pass_on(RING + k).wait_send()

    for j in range(1, 8):
        g_copy(j).wait_send()
        y_copy(j).wait_send()
        z_copy(j).wait_send()
        a_copy(j).wait_send()
    for j in range(1, 8):
        a_copy(j).wait_recv()


def place(out, grad_weight, grad_feats, to_out, to_weight, to_feats, held_out, held_weight, held_feats, sem):
    held = (held_out, held_weight, held_feats)
    inward = [pltpu.make_async_copy(src, dst, sem.at[i]) for i, (src, dst) in enumerate(zip((out, grad_weight, grad_feats), held))]
    outward = [pltpu.make_async_copy(src, dst, sem.at[i]) for i, (src, dst) in enumerate(zip(held, (to_out, to_weight, to_feats)))]
    for c in inward:
        c.start()
    for c, d in zip(inward, outward):
        c.wait()
        d.start()
    for d in outward:
        d.wait()


def per_device(feats, tile_weights, tile_rows, slot_count, degrees, weight, grad_out):
    rows = tile_rows[0, 0].T
    count = slot_count.reshape(1, COLS)
    vmem = pl.BlockSpec(memory_space=pltpu.VMEM)
    hbm = pl.BlockSpec(memory_space=pl.ANY)
    dma = pltpu.SemaphoreType.DMA
    block = (BLOCK, FEAT)
    out_shape = (
        jax.ShapeDtypeStruct((BLOCK, HID), BF16),
        jax.ShapeDtypeStruct((8, SLAB, HID), F32),
        jax.ShapeDtypeStruct((BLOCK, FEAT), F32),
    )
    results = pl.pallas_call(
        kernel,
        out_shape=out_shape,
        in_specs=[hbm] * 7,
        out_specs=(vmem, vmem, vmem),
        scratch_shapes=[
            pltpu.SMEM((N_TEAM, COLS), jnp.int32),
            pltpu.SMEM((SLOTS, COLS), jnp.int32),
            pltpu.SMEM((1, COLS), jnp.int32),
            pltpu.VMEM((N_TEAM, COLS), jnp.int32),
            pltpu.VMEM((SLOTS, COLS), jnp.int32),
            pltpu.VMEM((1, COLS), jnp.int32),
            pltpu.VMEM((N_CHIP, 1, BLOCK), jnp.int32),
            pltpu.VMEM((FEAT, HID), BF16),
            pltpu.VMEM((N_CHIP, BLOCK, HID), BF16),
            pltpu.VMEM((N_CHIP,) + block, BF16),
            pltpu.VMEM((COLS, SLOTS * BLOCK, BLOCK), BF16),
            pltpu.VMEM((COLS,) + block, BF16),
            pltpu.VMEM((N_TEAM + 1,) + block, BF16),
            pltpu.VMEM((COLS * HELD,) + block, F32),
            pltpu.VMEM((N_CHIP,) + block, BF16),
            pltpu.VMEM((N_CHIP,) + block, BF16),
            pltpu.VMEM(block, F32),
            pltpu.VMEM((N_CHIP,) + block, BF16),
            pltpu.VMEM((N_CHIP,) + block, BF16),
            pltpu.VMEM((RING,) + block, BF16),
            pltpu.VMEM((RING,) + block, BF16),
            pltpu.VMEM((RING,) + block, F32),
            pltpu.VMEM((RING,) + block, BF16),
            pltpu.VMEM((RING,) + block, BF16),
            pltpu.VMEM((8, SLAB, HID), F32),
            pltpu.VMEM((8, SLAB, HID), BF16),
            pltpu.VMEM((8, SLAB, HID), BF16),
            pltpu.VMEM((SLAB, HID), BF16),
            pltpu.VMEM((8, SLAB, HID), BF16),
            pltpu.VMEM((SLAB, HID), BF16),
            pltpu.VMEM((8, SLAB, HID), BF16),
            dma((8,)), dma, dma((COLS // 4,)),
            dma((8,)), dma((8,)), dma((8,)), dma((8,)), dma((8,)), dma((8,)), dma((8,)), dma((8,)),
            dma((16,)), dma((16,)), dma((16,)), dma((16,)), dma((16,)), dma((16,)),
            dma((16,)), dma((16,)), dma((8,)), dma((8,)), dma((8,)), dma((8,)), dma((8,)), dma((8,)),
            dma((8,)), dma((8,)), dma((8,)), dma((8,)), dma((8,)), dma((8,)),
        ],
        compiler_params=pltpu.CompilerParams(
            collective_id=0, has_side_effects=True, vmem_limit_bytes=60 * 1024 * 1024),
    )(
        rows, count, feats,
        tile_weights.reshape(COLS, SLOTS * BLOCK, BLOCK),
        degrees.reshape(1, BLOCK), weight, grad_out,
    )
    out, grad_weight, grad_feats = pl.pallas_call(
        place,
        out_shape=out_shape,
        in_specs=[hbm] * 3,
        out_specs=(hbm,) * 3,
        scratch_shapes=[pltpu.VMEM(o.shape, o.dtype) for o in out_shape] + [dma((3,))],
    )(*results)
    return out, grad_weight.reshape(BLOCK, HID), grad_feats


def solution(mesh):
    placed = (
        P(("team", "member"), None),
        P("team", "member", None, None, None, None),
        P("team", "member", None, None),
        P("team", "member", None),
        P(("member", "team")),
        P(),
        P(("member", "team"), None),
    )
    return jax.shard_map(
        per_device,
        mesh=mesh,
        in_specs=placed,
        out_specs=(P(("member", "team"), None), P(), P(("team", "member"), None)),
        check_vma=False,
    )
```

```python
import jax
import jax.numpy as jnp
from jax import lax
from jax.experimental import pallas as pl
from jax.experimental.pallas import tpu as pltpu
from jax.sharding import PartitionSpec as P

MESH = pl.DeviceIdType.MESH
F32 = jnp.float32
BF16 = jnp.bfloat16

N_TEAM, N_MEMBER, N_CHIP, RING = 32, 16, 16, 8
BLOCK, FEAT, HID, SLOTS = 128, 128, 256, 8
COLS = 16
HELD = SLOTS + 1
SLAB = BLOCK // 8
FAR, NEAR = (4, 3, 5), (6, 2, 7, 1)
SPLIT = 2


def kernel(row_hbm, count_hbm, feats_hbm, tiles_hbm, degrees_hbm, weight_hbm, grad_out_hbm,
           out, grad_weight, grad_feats,
           slot_of, row_of, count, slot_vec, row_vec, count_vec, deg_all, weight, g_all, q_t,
           tiles, x_all, s_all, prod, part_sum, from_sib, to_sib, own_part, to_team, from_team,
           to_bx, from_bx, held_b, to_member, from_member, gw_part, slab_out, slab_in, slab, y_in, slab_y, z_in,
           in_sem, slot_sem, tile_sem, x_send, x_recv, x2_send, x2_recv, c_send, c_recv, c2_send, c2_recv, d_send, d_recv,
           f_send, f_recv, cs_send, cs_recv,
           t_send, t_recv, bx_send, bx_recv, b_send, b_recv, g_send, g_recv, y_send, y_recv, z_send, z_recv,
           a_send, a_recv):
    t = lax.axis_index("team")
    m = lax.axis_index("member")
    core = lax.rem(t, 2)
    chip = t // 2
    z = lax.rem(chip, RING)
    x_lo = chip // RING
    y = lax.rem(m, RING)
    x_hi = m // RING
    sib = chip * 2 + 1 - core
    group = core + 2 * x_lo + 4 * x_hi

    def signal(team, member):
        pl.semaphore_signal(barrier, inc=1, device_id=(team, member), device_id_type=MESH)

    def copy(src, dst, send, recv, team, member):
        return pltpu.make_async_remote_copy(
            src_ref=src, dst_ref=dst, send_sem=send, recv_sem=recv,
            device_id=(team, member), device_id_type=MESH)

    def chip_peer(k):
        return lax.rem(chip + k, N_CHIP)

    def flip(j):
        c = 1 - core if j & 1 else core
        xl = 1 - x_lo if j & 2 else x_lo
        xh = 1 - x_hi if j & 4 else x_hi
        return (xl * RING + z) * 2 + c, xh * RING + y, c + 2 * xl + 4 * xh

    def y_at(k):
        return lax.rem(y + k, RING)

    def z_at(k):
        return lax.rem(z + k, RING)

    def tile_copy(c):
        part = pl.ds(c * 4, 4)
        return pltpu.make_async_copy(tiles_hbm.at[part], tiles.at[part], tile_sem.at[c])

    pairs = ((weight_hbm, weight), (grad_out_hbm, g_all.at[chip]), (degrees_hbm, deg_all.at[chip]),
             (row_hbm, row_vec), (count_hbm, count_vec), (feats_hbm, x_all.at[m]),
             (row_hbm, row_of), (count_hbm, count))
    inputs = [pltpu.make_async_copy(src, dst, in_sem.at[i]) for i, (src, dst) in enumerate(pairs)]
    slot_copy = pltpu.make_async_copy(slot_vec, slot_of, slot_sem)

    barrier = pltpu.get_barrier_semaphore()

    for k in FAR + NEAR:
        signal(t, x_hi * RING + y_at(k))
    signal(t, (1 - x_hi) * RING + y)

    @pl.loop(1, N_CHIP)
    def _(k):
        signal(chip_peer(k) * 2 + core, m)

    signal(sib, m)
    for j in (3, 5, 6, 7):
        to_t, to_m, _ = flip(j)
        signal(to_t, to_m)

    pl.semaphore_wait(barrier, RING + N_CHIP - 1 + 5)

    def x_slot(row, k):
        return row * RING + lax.rem(y - k + RING, RING)

    def x_copy(k):
        return copy(feats_hbm, x_all.at[m], x_send.at[k], x_recv.at[k], t, x_hi * RING + y_at(k))

    def x_swap():
        return copy(feats_hbm, x_all.at[m], x2_send.at[0], x2_recv.at[0], t, (1 - x_hi) * RING + y)

    def x_near(k):
        slot = x_slot(1 - x_hi, 0)
        return copy(x_all.at[slot], x_all.at[slot], x2_send.at[k], x2_recv.at[k], t, x_hi * RING + y_at(k))

    def x_far(k):
        slot = x_slot(x_hi, k)
        return copy(x_all.at[slot], x_all.at[slot], x2_send.at[k], x2_recv.at[k], t, (1 - x_hi) * RING + y)

    def c_slot(row, k):
        return row * RING + lax.rem(z - k + RING, RING)

    def c_copy(k):
        return copy(grad_out_hbm, g_all.at[chip], c_send.at[k], c_recv.at[k], (x_lo * RING + z_at(k)) * 2 + core, m)

    def c_relay(k):
        back, to = {3: (2, 1), 4: (2, 2), 5: (6, 7)}[k]
        slot = c_slot(x_lo, back)
        return copy(g_all.at[slot], g_all.at[slot], c_send.at[k], c_recv.at[k],
                    (x_lo * RING + z_at(to)) * 2 + core, m)

    def c_swap():
        return copy(grad_out_hbm, g_all.at[chip], c2_send.at[0], c2_recv.at[0], ((1 - x_lo) * RING + z) * 2 + core, m)

    def c_near(k):
        slot = c_slot(1 - x_lo, 0)
        return copy(g_all.at[slot], g_all.at[slot], c2_send.at[k], c2_recv.at[k],
                    (x_lo * RING + z_at(k)) * 2 + core, m)

    def c_far(k):
        slot = c_slot(x_lo, k)
        return copy(g_all.at[slot], g_all.at[slot], c2_send.at[k], c2_recv.at[k],
                    ((1 - x_lo) * RING + z) * 2 + core, m)

    def d_copy(k):
        return copy(degrees_hbm, deg_all.at[chip], d_send.at[k], d_recv.at[k], chip_peer(k) * 2 + core, m)

    def inv_root(q):
        return lax.rsqrt(deg_all[q].astype(F32))

    def pass_on(q):
        r = q * 2 + core
        return copy(s_all.at[r], s_all.at[r], f_send.at[q], f_recv.at[q], sib, m)

    def passed(q):
        r = q * 2 + 1 - core
        return copy(s_all.at[r], s_all.at[r], f_send.at[q], f_recv.at[q], sib, m)

    def project(row):
        first = row * RING
        scaled_t = lax.dot_general(weight[...], g_all[pl.ds(first, RING)].reshape(RING * BLOCK, HID),
                                   (((1,), (1,)), ((), ())), preferred_element_type=F32)
        for i in range(RING):
            q = first + i
            s_all[q * 2 + core] = (scaled_t[:, i * BLOCK:(i + 1) * BLOCK] * inv_root(q)).astype(BF16)
            pass_on(q).start()

    x_swap().start()
    for k in FAR + NEAR:
        x_copy(k).start()
    c_swap().start()
    for k in NEAR:
        c_copy(k).start()
    for c in inputs:
        c.start()
    for c in range(COLS // 4):
        tile_copy(c).start()

    @pl.loop(1, N_CHIP)
    def _(k):
        d_copy(k).start()

    for c in inputs:
        c.wait()
    row_ids = lax.broadcasted_iota(jnp.int32, (N_TEAM, COLS), 0)
    slots = jnp.full((N_TEAM, COLS), SLOTS, jnp.int32)
    for s in range(SLOTS):
        slots = jnp.where((row_vec[s:s + 1, :] == row_ids) & (s < count_vec[...]), s, slots)
    slot_vec[...] = slots
    slot_copy.start()

    s_all[N_TEAM] = jnp.zeros((FEAT, BLOCK), BF16)
    for c in range(COLS):
        prod[c * HELD + SLOTS] = jnp.zeros((BLOCK, FEAT), F32)
    for c in range(COLS // 4):
        tile_copy(c).wait()
    slot_copy.wait()

    def multiply(c):
        products = jnp.dot(tiles[c], x_all[c], preferred_element_type=F32)
        prod[pl.ds(c * HELD, SLOTS)] = products.reshape(SLOTS, BLOCK, FEAT)

    x_swap().wait_recv()
    for k in NEAR:
        x_near(k).start()
    multiply(m)
    multiply(x_slot(1 - x_hi, 0))
    for k in FAR:
        x_copy(k).wait_recv()
        x_far(k).start()
    c_swap().wait_recv()
    for k in (6, 2):
        c_copy(k).wait_recv()
    for k in FAR:
        c_relay(k).start()
    for k in NEAR:
        c_near(k).start()
    for k in FAR:
        multiply(x_slot(x_hi, k))
    for k in NEAR:
        x_copy(k).wait_recv()
        multiply(x_slot(x_hi, k))

    @pl.loop(1, N_CHIP)
    def _(k):
        d_copy(k).wait_recv()

    early = [x_slot(x_hi, k) for k in range(RING)] + [x_slot(1 - x_hi, 0)]

    @pl.loop(0, N_TEAM)
    def _(r):
        total = prod[early[0] * HELD + slot_of[r, early[0]]]
        for c in early[1:]:
            total = total + prod[c * HELD + slot_of[r, c]]
        part_sum[r] = total

    for k in NEAR:
        x_near(k).wait_recv()
        multiply(x_slot(1 - x_hi, k))
    for k in FAR:
        c_relay(k).wait_recv()
        c_far(k).start()
    for k in FAR:
        x_far(k).wait_recv()
        multiply(x_slot(1 - x_hi, k))

    late = [x_slot(1 - x_hi, k) for k in range(1, RING)]

    def row_sum(r):
        total = part_sum[r]
        for c in late:
            total = total + prod[c * HELD + slot_of[r, c]]
        return total

    def outward(i):
        return lax.rem(4 + ((i + 1) // 2) * (1 - 2 * lax.rem(i, 2)) + RING, RING)

    def cs_copy(q):
        return copy(to_sib.at[q], from_sib.at[q], cs_send.at[q], cs_recv.at[q], sib, m)

    def t_copy(k):
        return copy(to_team.at[k], from_team.at[k], t_send.at[k], t_recv.at[k],
                    chip_peer(k) * 2 + core, m)

    def for_sibling(q):
        to_sib[q] = row_sum(q * 2 + 1 - core).astype(BF16)
        cs_copy(q).start()

    def finish_block(q):
        mine = row_sum(q * 2 + core)
        cs_copy(q).wait_recv()
        total = mine + from_sib[q].astype(F32)
        q_t[q] = (jnp.transpose(total) * inv_root(q)).astype(BF16)
        return total

    def for_team(q):
        k = lax.rem(q - chip + N_CHIP, N_CHIP)
        to_team[k] = finish_block(q).astype(BF16)
        t_copy(k).start()

    @pl.loop(0, RING)
    def _(i):
        dz = z_at(outward(i))
        for_sibling((1 - x_lo) * RING + dz)
        for_sibling(x_lo * RING + dz)

    @pl.loop(0, RING - 1)
    def _(i):
        dz = z_at(outward(i))
        for_team((1 - x_lo) * RING + dz)
        for_team(x_lo * RING + dz)

    for_team((1 - x_lo) * RING + z)
    own_part[...] = finish_block(chip)

    for k in (7, 1):
        c_copy(k).wait_recv()

    def weight_part(row):
        first = row * RING
        return jnp.dot(jnp.concatenate([q_t[first + i] for i in range(RING)], axis=1),
                       g_all[pl.ds(first, RING)].reshape(RING * BLOCK, HID), preferred_element_type=F32)

    part = weight_part(x_lo)
    project(x_lo)
    for k in NEAR:
        c_near(k).wait_recv()
    for k in FAR:
        c_far(k).wait_recv()
    part = (part + weight_part(1 - x_lo)).reshape(8, SLAB, HID)
    gw_part[...] = part
    slab_out[...] = part.astype(BF16)

    def g_copy(j):
        to_t, to_m, to_g = flip(j)
        return copy(slab_out.at[to_g], slab_in.at[j], g_send.at[j], g_recv.at[j], to_t, to_m)

    for j in (7, 6, 5, 4, 3, 2, 1):
        g_copy(j).start()

    project(1 - x_lo)

    @pl.loop(0, N_CHIP)
    def _(q):
        passed(q).wait_recv()

    def column(c):
        picked = [s_all[jnp.where(s < count[0, c], row_of[s, c], N_TEAM)] for s in range(SLOTS)]
        return jnp.dot(jnp.concatenate(picked, axis=1), tiles[c], preferred_element_type=F32)

    def bx_copy(i):
        return copy(to_bx.at[i], from_bx.at[i], bx_send.at[i], bx_recv.at[i], t, (1 - x_hi) * RING + y)

    def b_copy(k):
        return copy(to_member.at[k], from_member.at[k], b_send.at[k], b_recv.at[k], t, x_hi * RING + y_at(k))

    @pl.loop(0, RING)
    def _(i):
        dy = y_at(outward(i))
        to_bx[dy] = column((1 - x_hi) * RING + dy).astype(BF16)
        bx_copy(dy).start()

    for j in range(1, 8):
        g_copy(j).wait_recv()
    part = gw_part[group]
    for j in range(1, 8):
        part = part + slab_in[j].astype(F32)
    slab[...] = part.astype(BF16)

    def y_copy(k):
        return copy(slab, y_in.at[k], y_send.at[k], y_recv.at[k], t, x_hi * RING + y_at(k))

    def z_copy(k):
        return copy(slab_y, z_in.at[k], z_send.at[k], z_recv.at[k], (x_lo * RING + z_at(k)) * 2 + core, m)

    for k in FAR + NEAR:
        y_copy(k).start()

    @pl.loop(0, RING)
    def _(i):
        dy = y_at(outward(i))
        held_b[dy] = column(x_hi * RING + dy)

    def for_member(i):
        k = outward(i)
        dy = y_at(k)
        bx_copy(dy).wait_recv()
        to_member[k] = (held_b[dy] + from_bx[dy].astype(F32)).astype(BF16)
        b_copy(k).start()

    pl.loop(0, SPLIT)(for_member)

    for k in range(1, RING):
        y_copy(k).wait_recv()
    for k in range(1, RING):
        part = part + y_in[k].astype(F32)
    slab_y[...] = part.astype(BF16)
    for k in FAR + NEAR:
        z_copy(k).start()
    pl.loop(SPLIT, RING - 1)(for_member)

    @pl.loop(1, N_CHIP)
    def _(k):
        t_copy(k).wait_recv()

    summed = own_part[...]
    for k in range(1, N_CHIP):
        summed = summed + from_team[k].astype(F32)
    inv_col = jnp.transpose(jnp.broadcast_to(inv_root(chip), (BLOCK, BLOCK)))
    aggregate = (summed * inv_col).astype(BF16)
    out[...] = jnp.dot(aggregate, weight[...], preferred_element_type=F32).astype(BF16)

    for k in range(1, RING):
        z_copy(k).wait_recv()
    part = slab_y[...].astype(F32)
    for k in range(1, RING):
        part = part + z_in[k].astype(F32)
    grad_weight[group] = part * (N_TEAM * N_MEMBER * BLOCK) ** (-0.5)

    def a_copy(j):
        to_t, to_m, _ = flip(j)
        return copy(grad_weight.at[group], grad_weight.at[group], a_send.at[j], a_recv.at[j], to_t, to_m)

    for j in (7, 6, 5, 4, 3, 2, 1):
        a_copy(j).start()

    bx_copy(y).wait_recv()
    own_col = held_b[y] + from_bx[y].astype(F32)
    for k in FAR + NEAR:
        b_copy(k).wait_recv()
        own_col = own_col + from_member[k].astype(F32)
    grad_feats[...] = jnp.transpose(own_col)

    @pl.loop(1, N_MEMBER)
    def _(k):
        t_copy(k).wait_send()
        d_copy(k).wait_send()

    @pl.loop(0, N_CHIP)
    def _(k):
        cs_copy(k).wait_send()

    @pl.loop(0, RING)
    def _(k):
        bx_copy(k).wait_send()

    @pl.loop(1, RING)
    def _(k):
        b_copy(k).wait_send()
        x_copy(k).wait_send()

    x_swap().wait_send()
    c_swap().wait_send()
    for k in NEAR:
        x_near(k).wait_send()
        c_near(k).wait_send()
        c_copy(k).wait_send()
    for k in FAR:
        x_far(k).wait_send()
        c_far(k).wait_send()
        c_relay(k).wait_send()

    @pl.loop(0, RING)
    def _(k):
        pass_on(k).wait_send()
        pass_on(RING + k).wait_send()

    for j in range(1, 8):
        g_copy(j).wait_send()
        y_copy(j).wait_send()
        z_copy(j).wait_send()
        a_copy(j).wait_send()
    for j in range(1, 8):
        a_copy(j).wait_recv()


def place(out, grad_weight, grad_feats, to_out, to_weight, to_feats, held_out, held_weight, held_feats, sem):
    held = (held_out, held_weight, held_feats)
    inward = [pltpu.make_async_copy(src, dst, sem.at[i]) for i, (src, dst) in enumerate(zip((out, grad_weight, grad_feats), held))]
    outward = [pltpu.make_async_copy(src, dst, sem.at[i]) for i, (src, dst) in enumerate(zip(held, (to_out, to_weight, to_feats)))]
    for c in inward:
        c.start()
    for c, d in zip(inward, outward):
        c.wait()
        d.start()
    for d in outward:
        d.wait()


def per_device(feats, tile_weights, tile_rows, slot_count, degrees, weight, grad_out):
    rows = tile_rows[0, 0].T
    count = slot_count.reshape(1, COLS)
    vmem = pl.BlockSpec(memory_space=pltpu.VMEM)
    hbm = pl.BlockSpec(memory_space=pl.ANY)
    dma = pltpu.SemaphoreType.DMA
    block = (BLOCK, FEAT)
    out_shape = (
        jax.ShapeDtypeStruct((BLOCK, HID), BF16),
        jax.ShapeDtypeStruct((8, SLAB, HID), F32),
        jax.ShapeDtypeStruct((BLOCK, FEAT), F32),
    )
    results = pl.pallas_call(
        kernel,
        out_shape=out_shape,
        in_specs=[hbm] * 7,
        out_specs=(vmem, vmem, vmem),
        scratch_shapes=[
            pltpu.SMEM((N_TEAM, COLS), jnp.int32),
            pltpu.SMEM((SLOTS, COLS), jnp.int32),
            pltpu.SMEM((1, COLS), jnp.int32),
            pltpu.VMEM((N_TEAM, COLS), jnp.int32),
            pltpu.VMEM((SLOTS, COLS), jnp.int32),
            pltpu.VMEM((1, COLS), jnp.int32),
            pltpu.VMEM((N_CHIP, 1, BLOCK), jnp.int32),
            pltpu.VMEM((FEAT, HID), BF16),
            pltpu.VMEM((N_CHIP, BLOCK, HID), BF16),
            pltpu.VMEM((N_CHIP,) + block, BF16),
            pltpu.VMEM((COLS, SLOTS * BLOCK, BLOCK), BF16),
            pltpu.VMEM((COLS,) + block, BF16),
            pltpu.VMEM((N_TEAM + 1,) + block, BF16),
            pltpu.VMEM((COLS * HELD,) + block, F32),
            pltpu.VMEM((N_TEAM,) + block, F32),
            pltpu.VMEM((N_CHIP,) + block, BF16),
            pltpu.VMEM((N_CHIP,) + block, BF16),
            pltpu.VMEM(block, F32),
            pltpu.VMEM((N_CHIP,) + block, BF16),
            pltpu.VMEM((N_CHIP,) + block, BF16),
            pltpu.VMEM((RING,) + block, BF16),
            pltpu.VMEM((RING,) + block, BF16),
            pltpu.VMEM((RING,) + block, F32),
            pltpu.VMEM((RING,) + block, BF16),
            pltpu.VMEM((RING,) + block, BF16),
            pltpu.VMEM((8, SLAB, HID), F32),
            pltpu.VMEM((8, SLAB, HID), BF16),
            pltpu.VMEM((8, SLAB, HID), BF16),
            pltpu.VMEM((SLAB, HID), BF16),
            pltpu.VMEM((8, SLAB, HID), BF16),
            pltpu.VMEM((SLAB, HID), BF16),
            pltpu.VMEM((8, SLAB, HID), BF16),
            dma((8,)), dma, dma((COLS // 4,)),
            dma((8,)), dma((8,)), dma((8,)), dma((8,)), dma((8,)), dma((8,)), dma((8,)), dma((8,)),
            dma((16,)), dma((16,)), dma((16,)), dma((16,)), dma((16,)), dma((16,)),
            dma((16,)), dma((16,)), dma((8,)), dma((8,)), dma((8,)), dma((8,)), dma((8,)), dma((8,)),
            dma((8,)), dma((8,)), dma((8,)), dma((8,)), dma((8,)), dma((8,)),
        ],
        compiler_params=pltpu.CompilerParams(
            collective_id=0, has_side_effects=True, vmem_limit_bytes=60 * 1024 * 1024),
    )(
        rows, count, feats,
        tile_weights.reshape(COLS, SLOTS * BLOCK, BLOCK),
        degrees.reshape(1, BLOCK), weight, grad_out,
    )
    out, grad_weight, grad_feats = pl.pallas_call(
        place,
        out_shape=out_shape,
        in_specs=[hbm] * 3,
        out_specs=(hbm,) * 3,
        scratch_shapes=[pltpu.VMEM(o.shape, o.dtype) for o in out_shape] + [dma((3,))],
    )(*results)
    return out, grad_weight.reshape(BLOCK, HID), grad_feats


def solution(mesh):
    placed = (
        P(("team", "member"), None),
        P("team", "member", None, None, None, None),
        P("team", "member", None, None),
        P("team", "member", None),
        P(("member", "team")),
        P(),
        P(("member", "team"), None),
    )
    return jax.shard_map(
        per_device,
        mesh=mesh,
        in_specs=placed,
        out_specs=(P(("member", "team"), None), P(), P(("team", "member"), None)),
        check_vma=False,
    )
```

```python
import jax
import jax.numpy as jnp
from jax import lax
from jax.experimental import pallas as pl
from jax.experimental.pallas import tpu as pltpu
from jax.sharding import PartitionSpec as P

MESH = pl.DeviceIdType.MESH
F32 = jnp.float32
BF16 = jnp.bfloat16

N_TEAM, N_MEMBER, N_CHIP, RING = 32, 16, 16, 8
BLOCK, FEAT, HID, SLOTS = 128, 128, 256, 8
COLS = 16
HELD = SLOTS + 1
SLAB = BLOCK // 8
FAR, NEAR = (4, 3, 5), (6, 2, 7, 1)
SPLIT = 2


def kernel(row_hbm, count_hbm, feats_hbm, tiles_hbm, degrees_hbm, weight_hbm, grad_out_hbm,
           out, grad_weight, grad_feats,
           slot_of, row_of, count, slot_vec, row_vec, count_vec, deg_all, weight, g_all, q_t,
           tiles, x_all, s_all, prod, part_sum, from_sib, to_sib, own_part, to_team, from_team,
           to_bx, from_bx, held_b, to_member, from_member, gw_part, slab_out, slab_in, slab, y_in, slab_y, z_in,
           in_sem, slot_sem, tile_sem, x_send, x_recv, x2_send, x2_recv, c_send, c_recv, c2_send, c2_recv, d_send, d_recv,
           f_send, f_recv, cs_send, cs_recv,
           t_send, t_recv, bx_send, bx_recv, b_send, b_recv, g_send, g_recv, y_send, y_recv, z_send, z_recv,
           a_send, a_recv):
    t = lax.axis_index("team")
    m = lax.axis_index("member")
    core = lax.rem(t, 2)
    chip = t // 2
    z = lax.rem(chip, RING)
    x_lo = chip // RING
    y = lax.rem(m, RING)
    x_hi = m // RING
    sib = chip * 2 + 1 - core
    group = core + 2 * x_lo + 4 * x_hi

    def signal(team, member):
        pl.semaphore_signal(barrier, inc=1, device_id=(team, member), device_id_type=MESH)

    def copy(src, dst, send, recv, team, member):
        return pltpu.make_async_remote_copy(
            src_ref=src, dst_ref=dst, send_sem=send, recv_sem=recv,
            device_id=(team, member), device_id_type=MESH)

    def chip_peer(k):
        return lax.rem(chip + k, N_CHIP)

    def flip(j):
        c = 1 - core if j & 1 else core
        xl = 1 - x_lo if j & 2 else x_lo
        xh = 1 - x_hi if j & 4 else x_hi
        return (xl * RING + z) * 2 + c, xh * RING + y, c + 2 * xl + 4 * xh

    def y_at(k):
        return lax.rem(y + k, RING)

    def z_at(k):
        return lax.rem(z + k, RING)

    def tile_copy(c):
        part = pl.ds(c * 4, 4)
        return pltpu.make_async_copy(tiles_hbm.at[part], tiles.at[part], tile_sem.at[c])

    pairs = ((weight_hbm, weight), (grad_out_hbm, g_all.at[chip]), (degrees_hbm, deg_all.at[chip]),
             (row_hbm, row_vec), (count_hbm, count_vec), (feats_hbm, x_all.at[m]),
             (row_hbm, row_of), (count_hbm, count))
    inputs = [pltpu.make_async_copy(src, dst, in_sem.at[i]) for i, (src, dst) in enumerate(pairs)]
    slot_copy = pltpu.make_async_copy(slot_vec, slot_of, slot_sem)

    barrier = pltpu.get_barrier_semaphore()

    for k in FAR + NEAR:
        signal(t, x_hi * RING + y_at(k))
    signal(t, (1 - x_hi) * RING + y)

    @pl.loop(1, N_CHIP)
    def _(k):
        signal(chip_peer(k) * 2 + core, m)

    signal(sib, m)
    for j in (3, 5, 6, 7):
        to_t, to_m, _ = flip(j)
        signal(to_t, to_m)

    pl.semaphore_wait(barrier, RING + N_CHIP - 1 + 5)

    def x_slot(row, k):
        return row * RING + lax.rem(y - k + RING, RING)

    def x_copy(k):
        return copy(feats_hbm, x_all.at[m], x_send.at[k], x_recv.at[k], t, x_hi * RING + y_at(k))

    def x_swap():
        return copy(feats_hbm, x_all.at[m], x2_send.at[0], x2_recv.at[0], t, (1 - x_hi) * RING + y)

    def x_near(k):
        slot = x_slot(1 - x_hi, 0)
        return copy(x_all.at[slot], x_all.at[slot], x2_send.at[k], x2_recv.at[k], t, x_hi * RING + y_at(k))

    def x_far(k):
        slot = x_slot(x_hi, k)
        return copy(x_all.at[slot], x_all.at[slot], x2_send.at[k], x2_recv.at[k], t, (1 - x_hi) * RING + y)

    def c_slot(row, k):
        return row * RING + lax.rem(z - k + RING, RING)

    def c_copy(k):
        return copy(grad_out_hbm, g_all.at[chip], c_send.at[k], c_recv.at[k], (x_lo * RING + z_at(k)) * 2 + core, m)

    def c_relay(k):
        back, to = {3: (2, 1), 4: (2, 2), 5: (6, 7)}[k]
        slot = c_slot(x_lo, back)
        return copy(g_all.at[slot], g_all.at[slot], c_send.at[k], c_recv.at[k],
                    (x_lo * RING + z_at(to)) * 2 + core, m)

    def c_swap():
        return copy(grad_out_hbm, g_all.at[chip], c2_send.at[0], c2_recv.at[0], ((1 - x_lo) * RING + z) * 2 + core, m)

    def c_near(k):
        slot = c_slot(1 - x_lo, 0)
        return copy(g_all.at[slot], g_all.at[slot], c2_send.at[k], c2_recv.at[k],
                    (x_lo * RING + z_at(k)) * 2 + core, m)

    def c_far(k):
        slot = c_slot(x_lo, k)
        return copy(g_all.at[slot], g_all.at[slot], c2_send.at[k], c2_recv.at[k],
                    ((1 - x_lo) * RING + z) * 2 + core, m)

    def d_copy(k):
        return copy(degrees_hbm, deg_all.at[chip], d_send.at[k], d_recv.at[k], chip_peer(k) * 2 + core, m)

    def inv_root(q):
        return lax.rsqrt(deg_all[q].astype(F32))

    def pass_on(q):
        r = q * 2 + core
        return copy(s_all.at[r], s_all.at[r], f_send.at[q], f_recv.at[q], sib, m)

    def passed(q):
        r = q * 2 + 1 - core
        return copy(s_all.at[r], s_all.at[r], f_send.at[q], f_recv.at[q], sib, m)

    def project(row):
        first = row * RING
        scaled_t = lax.dot_general(weight[...], g_all[pl.ds(first, RING)].reshape(RING * BLOCK, HID),
                                   (((1,), (1,)), ((), ())), preferred_element_type=F32)
        for i in range(RING):
            q = first + i
            s_all[q * 2 + core] = (scaled_t[:, i * BLOCK:(i + 1) * BLOCK] * inv_root(q)).astype(BF16)
            pass_on(q).start()

    for k in (6, 2):
        c_copy(k).start()
    x_swap().start()
    for k in FAR + NEAR:
        x_copy(k).start()
    for k in (7, 1):
        c_copy(k).start()
    c_swap().start()
    for c in inputs:
        c.start()
    for c in range(COLS // 4):
        tile_copy(c).start()

    @pl.loop(1, N_CHIP)
    def _(k):
        d_copy(k).start()

    for c in inputs:
        c.wait()
    row_ids = lax.broadcasted_iota(jnp.int32, (N_TEAM, COLS), 0)
    slots = jnp.full((N_TEAM, COLS), SLOTS, jnp.int32)
    for s in range(SLOTS):
        slots = jnp.where((row_vec[s:s + 1, :] == row_ids) & (s < count_vec[...]), s, slots)
    slot_vec[...] = slots
    slot_copy.start()

    s_all[N_TEAM] = jnp.zeros((FEAT, BLOCK), BF16)
    for c in range(COLS):
        prod[c * HELD + SLOTS] = jnp.zeros((BLOCK, FEAT), F32)
    for c in range(COLS // 4):
        tile_copy(c).wait()
    slot_copy.wait()

    def multiply(c):
        products = jnp.dot(tiles[c], x_all[c], preferred_element_type=F32)
        prod[pl.ds(c * HELD, SLOTS)] = products.reshape(SLOTS, BLOCK, FEAT)

    x_swap().wait_recv()
    for k in NEAR:
        x_near(k).start()
    multiply(m)
    multiply(x_slot(1 - x_hi, 0))
    for k in FAR:
        x_copy(k).wait_recv()
        x_far(k).start()
    c_swap().wait_recv()
    for k in (6, 2):
        c_copy(k).wait_recv()
    for k in FAR:
        c_relay(k).start()
    for k in NEAR:
        c_near(k).start()
    for k in FAR:
        multiply(x_slot(x_hi, k))
    for k in NEAR:
        x_copy(k).wait_recv()
        multiply(x_slot(x_hi, k))

    @pl.loop(1, N_CHIP)
    def _(k):
        d_copy(k).wait_recv()

    early = [x_slot(x_hi, k) for k in range(RING)] + [x_slot(1 - x_hi, 0)]

    @pl.loop(0, N_TEAM)
    def _(r):
        total = prod[early[0] * HELD + slot_of[r, early[0]]]
        for c in early[1:]:
            total = total + prod[c * HELD + slot_of[r, c]]
        part_sum[r] = total

    for k in NEAR:
        x_near(k).wait_recv()
        multiply(x_slot(1 - x_hi, k))
    for k in FAR:
        c_relay(k).wait_recv()
        c_far(k).start()
    for k in FAR:
        x_far(k).wait_recv()
        multiply(x_slot(1 - x_hi, k))

    late = [x_slot(1 - x_hi, k) for k in range(1, RING)]

    def row_sum(r):
        total = part_sum[r]
        for c in late:
            total = total + prod[c * HELD + slot_of[r, c]]
        return total

    def outward(i):
        return lax.rem(4 + ((i + 1) // 2) * (1 - 2 * lax.rem(i, 2)) + RING, RING)

    def cs_copy(q):
        return copy(to_sib.at[q], from_sib.at[q], cs_send.at[q], cs_recv.at[q], sib, m)

    def t_copy(k):
        return copy(to_team.at[k], from_team.at[k], t_send.at[k], t_recv.at[k],
                    chip_peer(k) * 2 + core, m)

    def for_sibling(q):
        to_sib[q] = row_sum(q * 2 + 1 - core).astype(BF16)
        cs_copy(q).start()

    def finish_block(q):
        mine = row_sum(q * 2 + core)
        cs_copy(q).wait_recv()
        total = mine + from_sib[q].astype(F32)
        q_t[q] = (jnp.transpose(total) * inv_root(q)).astype(BF16)
        return total

    def for_team(q):
        k = lax.rem(q - chip + N_CHIP, N_CHIP)
        to_team[k] = finish_block(q).astype(BF16)
        t_copy(k).start()

    @pl.loop(0, RING)
    def _(i):
        dz = z_at(outward(i))
        for_sibling((1 - x_lo) * RING + dz)
        for_sibling(x_lo * RING + dz)

    @pl.loop(0, RING - 1)
    def _(i):
        dz = z_at(outward(i))
        for_team((1 - x_lo) * RING + dz)
        for_team(x_lo * RING + dz)

    for_team((1 - x_lo) * RING + z)
    own_part[...] = finish_block(chip)

    for k in (7, 1):
        c_copy(k).wait_recv()

    def weight_part(row):
        first = row * RING
        return jnp.dot(jnp.concatenate([q_t[first + i] for i in range(RING)], axis=1),
                       g_all[pl.ds(first, RING)].reshape(RING * BLOCK, HID), preferred_element_type=F32)

    part = weight_part(x_lo)
    project(x_lo)
    for k in NEAR:
        c_near(k).wait_recv()
    for k in FAR:
        c_far(k).wait_recv()
    part = (part + weight_part(1 - x_lo)).reshape(8, SLAB, HID)
    gw_part[...] = part
    slab_out[...] = part.astype(BF16)

    def g_copy(j):
        to_t, to_m, to_g = flip(j)
        return copy(slab_out.at[to_g], slab_in.at[j], g_send.at[j], g_recv.at[j], to_t, to_m)

    for j in (7, 6, 5, 4, 3, 2, 1):
        g_copy(j).start()

    project(1 - x_lo)

    @pl.loop(0, N_CHIP)
    def _(q):
        passed(q).wait_recv()

    def column(c):
        picked = [s_all[jnp.where(s < count[0, c], row_of[s, c], N_TEAM)] for s in range(SLOTS)]
        return jnp.dot(jnp.concatenate(picked, axis=1), tiles[c], preferred_element_type=F32)

    def bx_copy(i):
        return copy(to_bx.at[i], from_bx.at[i], bx_send.at[i], bx_recv.at[i], t, (1 - x_hi) * RING + y)

    def b_copy(k):
        return copy(to_member.at[k], from_member.at[k], b_send.at[k], b_recv.at[k], t, x_hi * RING + y_at(k))

    def for_other(i):
        dy = y_at(outward(i))
        to_bx[dy] = column((1 - x_hi) * RING + dy).astype(BF16)
        bx_copy(dy).start()

    pl.loop(0, 4)(for_other)

    for j in range(1, 8):
        g_copy(j).wait_recv()
    part = gw_part[group]
    for j in range(1, 8):
        part = part + slab_in[j].astype(F32)
    slab[...] = part.astype(BF16)

    def y_copy(k):
        return copy(slab, y_in.at[k], y_send.at[k], y_recv.at[k], t, x_hi * RING + y_at(k))

    def z_copy(k):
        return copy(slab_y, z_in.at[k], z_send.at[k], z_recv.at[k], (x_lo * RING + z_at(k)) * 2 + core, m)

    for k in FAR + NEAR:
        y_copy(k).start()

    pl.loop(4, RING)(for_other)

    @pl.loop(0, RING)
    def _(i):
        dy = y_at(outward(i))
        held_b[dy] = column(x_hi * RING + dy)

    def for_member(i):
        k = outward(i)
        dy = y_at(k)
        bx_copy(dy).wait_recv()
        to_member[k] = (held_b[dy] + from_bx[dy].astype(F32)).astype(BF16)
        b_copy(k).start()

    pl.loop(0, SPLIT)(for_member)

    for k in range(1, RING):
        y_copy(k).wait_recv()
    for k in range(1, RING):
        part = part + y_in[k].astype(F32)
    slab_y[...] = part.astype(BF16)
    for k in FAR + NEAR:
        z_copy(k).start()
    pl.loop(SPLIT, RING - 1)(for_member)

    @pl.loop(1, N_CHIP)
    def _(k):
        t_copy(k).wait_recv()

    summed = own_part[...]
    for k in range(1, N_CHIP):
        summed = summed + from_team[k].astype(F32)
    inv_col = jnp.transpose(jnp.broadcast_to(inv_root(chip), (BLOCK, BLOCK)))
    aggregate = (summed * inv_col).astype(BF16)
    out[...] = jnp.dot(aggregate, weight[...], preferred_element_type=F32).astype(BF16)

    for k in range(1, RING):
        z_copy(k).wait_recv()
    part = slab_y[...].astype(F32)
    for k in range(1, RING):
        part = part + z_in[k].astype(F32)
    grad_weight[group] = part * (N_TEAM * N_MEMBER * BLOCK) ** (-0.5)

    def a_copy(j):
        to_t, to_m, _ = flip(j)
        return copy(grad_weight.at[group], grad_weight.at[group], a_send.at[j], a_recv.at[j], to_t, to_m)

    for j in (7, 6, 5, 4, 3, 2, 1):
        a_copy(j).start()

    bx_copy(y).wait_recv()
    own_col = held_b[y] + from_bx[y].astype(F32)
    for k in FAR + NEAR:
        b_copy(k).wait_recv()
        own_col = own_col + from_member[k].astype(F32)
    grad_feats[...] = jnp.transpose(own_col)

    @pl.loop(1, N_MEMBER)
    def _(k):
        t_copy(k).wait_send()
        d_copy(k).wait_send()

    @pl.loop(0, N_CHIP)
    def _(k):
        cs_copy(k).wait_send()

    @pl.loop(0, RING)
    def _(k):
        bx_copy(k).wait_send()

    @pl.loop(1, RING)
    def _(k):
        b_copy(k).wait_send()
        x_copy(k).wait_send()

    x_swap().wait_send()
    c_swap().wait_send()
    for k in NEAR:
        x_near(k).wait_send()
        c_near(k).wait_send()
        c_copy(k).wait_send()
    for k in FAR:
        x_far(k).wait_send()
        c_far(k).wait_send()
        c_relay(k).wait_send()

    @pl.loop(0, RING)
    def _(k):
        pass_on(k).wait_send()
        pass_on(RING + k).wait_send()

    for j in range(1, 8):
        g_copy(j).wait_send()
        y_copy(j).wait_send()
        z_copy(j).wait_send()
        a_copy(j).wait_send()
    for j in range(1, 8):
        a_copy(j).wait_recv()


def place(out, grad_weight, grad_feats, to_out, to_weight, to_feats, sem):
    pairs = ((out, to_out), (grad_weight, to_weight), (grad_feats, to_feats))
    copies = [pltpu.make_async_copy(src, dst, sem.at[i]) for i, (src, dst) in enumerate(pairs)]
    for c in copies:
        c.start()
    for c in copies:
        c.wait()


def per_device(feats, tile_weights, tile_rows, slot_count, degrees, weight, grad_out):
    rows = tile_rows[0, 0].T
    count = slot_count.reshape(1, COLS)
    vmem = pl.BlockSpec(memory_space=pltpu.VMEM)
    hbm = pl.BlockSpec(memory_space=pl.ANY)
    dma = pltpu.SemaphoreType.DMA
    block = (BLOCK, FEAT)
    out_shape = (
        jax.ShapeDtypeStruct((BLOCK, HID), BF16),
        jax.ShapeDtypeStruct((8, SLAB, HID), F32),
        jax.ShapeDtypeStruct((BLOCK, FEAT), F32),
    )
    results = pl.pallas_call(
        kernel,
        out_shape=out_shape,
        in_specs=[hbm] * 7,
        out_specs=(vmem, vmem, vmem),
        scratch_shapes=[
            pltpu.SMEM((N_TEAM, COLS), jnp.int32),
            pltpu.SMEM((SLOTS, COLS), jnp.int32),
            pltpu.SMEM((1, COLS), jnp.int32),
            pltpu.VMEM((N_TEAM, COLS), jnp.int32),
            pltpu.VMEM((SLOTS, COLS), jnp.int32),
            pltpu.VMEM((1, COLS), jnp.int32),
            pltpu.VMEM((N_CHIP, 1, BLOCK), jnp.int32),
            pltpu.VMEM((FEAT, HID), BF16),
            pltpu.VMEM((N_CHIP, BLOCK, HID), BF16),
            pltpu.VMEM((N_CHIP,) + block, BF16),
            pltpu.VMEM((COLS, SLOTS * BLOCK, BLOCK), BF16),
            pltpu.VMEM((COLS,) + block, BF16),
            pltpu.VMEM((N_TEAM + 1,) + block, BF16),
            pltpu.VMEM((COLS * HELD,) + block, F32),
            pltpu.VMEM((N_TEAM,) + block, F32),
            pltpu.VMEM((N_CHIP,) + block, BF16),
            pltpu.VMEM((N_CHIP,) + block, BF16),
            pltpu.VMEM(block, F32),
            pltpu.VMEM((N_CHIP,) + block, BF16),
            pltpu.VMEM((N_CHIP,) + block, BF16),
            pltpu.VMEM((RING,) + block, BF16),
            pltpu.VMEM((RING,) + block, BF16),
            pltpu.VMEM((RING,) + block, F32),
            pltpu.VMEM((RING,) + block, BF16),
            pltpu.VMEM((RING,) + block, BF16),
            pltpu.VMEM((8, SLAB, HID), F32),
            pltpu.VMEM((8, SLAB, HID), BF16),
            pltpu.VMEM((8, SLAB, HID), BF16),
            pltpu.VMEM((SLAB, HID), BF16),
            pltpu.VMEM((8, SLAB, HID), BF16),
            pltpu.VMEM((SLAB, HID), BF16),
            pltpu.VMEM((8, SLAB, HID), BF16),
            dma((8,)), dma, dma((COLS // 4,)),
            dma((8,)), dma((8,)), dma((8,)), dma((8,)), dma((8,)), dma((8,)), dma((8,)), dma((8,)),
            dma((16,)), dma((16,)), dma((16,)), dma((16,)), dma((16,)), dma((16,)),
            dma((16,)), dma((16,)), dma((8,)), dma((8,)), dma((8,)), dma((8,)), dma((8,)), dma((8,)),
            dma((8,)), dma((8,)), dma((8,)), dma((8,)), dma((8,)), dma((8,)),
        ],
        compiler_params=pltpu.CompilerParams(
            collective_id=0, has_side_effects=True, vmem_limit_bytes=60 * 1024 * 1024),
    )(
        rows, count, feats,
        tile_weights.reshape(COLS, SLOTS * BLOCK, BLOCK),
        degrees.reshape(1, BLOCK), weight, grad_out,
    )
    out, grad_weight, grad_feats = pl.pallas_call(
        place,
        out_shape=out_shape,
        in_specs=[vmem] * 3,
        out_specs=(hbm,) * 3,
        scratch_shapes=[dma((3,))],
    )(*results)
    return out, grad_weight.reshape(BLOCK, HID), grad_feats


def solution(mesh):
    placed = (
        P(("team", "member"), None),
        P("team", "member", None, None, None, None),
        P("team", "member", None, None),
        P("team", "member", None),
        P(("member", "team")),
        P(),
        P(("member", "team"), None),
    )
    return jax.shard_map(
        per_device,
        mesh=mesh,
        in_specs=placed,
        out_specs=(P(("member", "team"), None), P(), P(("team", "member"), None)),
        check_vma=False,
    )
```
